32 devices in a mesh: tm: 8 (over z, y), chan: 4 (over x, core).
Axes of the slice: x: 2, y: 2, z: 4, core: 2. Of those that a mesh axis runs over, the one named last changes fastest.
Arguments:
- signals: bfloat16 [32768, 2048], P('tm', 'chan')
- channel_node: int32 [2048], P('chan'), may hold values from 0 to 127, as said below
- lag_offsets: int32 [8], replicated, may hold values from 0 to 512, as said below
Outputs:
- r_factor: float32 [1024, 1024], replicated
The draws below stay inside these ranges and needn't reach their ends.
Inputs may be any that keep to these rules, and one draw needn't show every extreme that they name: `channel_node`: every node is named by exactly 16 channels; which channels, and so which channel groups, is drawn. `lag_offsets`: strictly increasing; the first is 0 and the last is 512.
All inputs are finite; a program needn't handle non-finite values.
Results may differ from the reference program's by a relative error of at most 0.0003.
Values sent between devices are 32-bit elements; how exact they have to be, the bound alone decides.
No kernel may reach another device: no remote copies, remote signals or barrier semaphores. Data moves between devices by JAX's collectives and lax.ppermute only.
A program may use at most 64 MiB of HBM per device.

```python
import math
import jax
import jax.numpy as jnp
from jax import lax

K = 1024
NODES = 128
CH = 2048
MAXLAG = 512
MODES = 6
TR = 4096
LAGS = 8
TIME = 32768
N_CHAN = 4


def draw_signals(key, part):
    keys = jax.random.split(key, 5)
    period = 4096
    times = jnp.arange(TIME, dtype=jnp.int32)[:, None] % period
    freqs = jax.random.randint(keys[0], (MODES,), 1, 1024)
    phases = jax.random.uniform(keys[1], (MODES,), jnp.float32, 0.0, 2.0 * math.pi)
    shapes = jax.random.normal(keys[2], (MODES, CH), jnp.float32) * 0.35
    scales = jnp.exp(jax.random.uniform(keys[3], (1, CH), jnp.float32, 0.0, math.log(10.0)))
    rows = jnp.arange(TIME, dtype=jnp.int32)[:, None].astype(jnp.float32)
    modal = jnp.zeros((TIME, CH), jnp.float32)
    for mode in range(MODES):
        index = times * freqs[mode] % period
        wave = jnp.sin(index.astype(jnp.float32) * (2.0 * math.pi / period) + phases[mode])
        modal = modal + wave * shapes[mode][None, :]
    noise = jax.random.normal(keys[4], (TIME, CH), jnp.float32)
    envelope = 1.0 + 2.0 * rows / TIME
    base = noise + modal
    return (base * envelope * scales * 0.3).astype(jnp.bfloat16)


def draw_channel_node(key, part):
    order = jax.random.permutation(key, CH)
    return (order % NODES).astype(jnp.int32)


def draw_lag_offsets(key, part):
    inner = jax.random.permutation(key, MAXLAG - 1)[:LAGS - 2] + 1
    inner = jnp.sort(inner.astype(jnp.int32))
    return jnp.concatenate([jnp.zeros((1,), jnp.int32), inner, jnp.full((1,), MAXLAG, jnp.int32)])


def setup_inputs(seed: int = 0) -> dict:
    arg_keys = jax.random.split(jax.random.key(seed), 4)
    return {
        "signals": draw_signals(jax.random.fold_in(arg_keys[3], 71), 0),
        "channel_node": draw_channel_node(jax.random.fold_in(arg_keys[3], 71), 0),
        "lag_offsets": draw_lag_offsets(jax.random.fold_in(arg_keys[3], 71), 0),
    }


def reference(signals, channel_node, lag_offsets):
    group_width = NODES // N_CHAN
    lag_count = K // NODES
    block_rows = TR // N_CHAN
    block_total = TIME // block_rows
    onehot = (channel_node[:, None] == jnp.arange(NODES, dtype=jnp.int32)[None, :]).astype(jnp.float32)
    node_scale = 1.0 / math.sqrt(CH // NODES)

    def node_block(rows_in):
        return jnp.dot(rows_in.astype(jnp.float32), onehot.astype(jnp.float32), precision=lax.Precision.HIGHEST, preferred_element_type=jnp.float32)
    node_signals = lax.map(node_block, signals.reshape(block_total, block_rows, CH)).reshape(TIME, NODES) * node_scale
    padded = jnp.concatenate([node_signals, jnp.zeros((MAXLAG, NODES), jnp.float32)], axis=0)

    def add_block(block_index, gram_matrix):
        row_start = (block_index * block_rows).astype(jnp.int32)
        columns = []
        for group in range(N_CHAN):
            for lag_index in range(lag_count):
                first = (row_start + lag_offsets[lag_index]).astype(jnp.int32)
                columns.append(lax.dynamic_slice(padded, (first, jnp.int32(group * group_width)), (block_rows, group_width)))
        hankel = jnp.concatenate(columns, axis=1)
        return gram_matrix + lax.dot_general(hankel.astype(jnp.float32), hankel.astype(jnp.float32), (((0,), (0,)), ((), ())), precision=lax.Precision.HIGHEST, preferred_element_type=jnp.float32)
    gram_matrix = lax.fori_loop(0, block_total, add_block, jnp.zeros((K, K), jnp.float32))
    gram_matrix = gram_matrix / TIME
    return jnp.linalg.cholesky(gram_matrix).T
```

```python
import functools
import math

import jax
import jax.numpy as jnp
from jax import lax
from jax.experimental import pallas as pl
from jax.experimental.pallas import tpu as pltpu
from jax.sharding import PartitionSpec as P

NODES = 128
CH = 2048
MAXLAG = 512
BLOCK = 128
GROUP = 8
HIGHEST = lax.Precision.HIGHEST
CONTRACT_ROWS = (((0,), (0,)), ((), ()))


def swap(value, axis, bit):
    count = lax.axis_size(axis)
    return lax.ppermute(value, axis, [(i, i ^ bit) for i in range(count)])


def bits_of(axis):
    count = lax.axis_size(axis)
    return [1 << i for i in range(count.bit_length() - 1)]


def halve(value, axis, bit):
    half = value.shape[0] // 2
    mine = (lax.axis_index(axis) // bit) % 2
    send = lax.dynamic_slice_in_dim(value, (1 - mine) * half, half, 0)
    keep = lax.dynamic_slice_in_dim(value, mine * half, half, 0)
    return keep + swap(send, axis, bit)


def scatter_rows(value, axis):
    bits = bits_of(axis)
    parts = value.reshape((2,) * len(bits) + (value.shape[0] >> len(bits), value.shape[1]))
    for place, bit in enumerate(bits):
        dim = len(bits) - 1 - place
        mine = (lax.axis_index(axis) // bit) % 2
        send = lax.dynamic_index_in_dim(parts, 1 - mine, dim, keepdims=False)
        keep = lax.dynamic_index_in_dim(parts, mine, dim, keepdims=False)
        parts = keep + swap(send, axis, bit)
    return parts


def double(value, axis, bit):
    mine = (lax.axis_index(axis) // bit) % 2
    other = swap(value, axis, bit)
    low = jnp.where(mine == 0, value, other)
    high = jnp.where(mine == 0, other, value)
    return jnp.concatenate([low, high], axis=0)


def sum_over_devices(value):
    stages = [(axis, bit) for axis in ("chan", "tm") for bit in bits_of(axis)]
    rows = value.shape[0]
    padded = -rows % (1 << len(stages))
    if padded:
        value = jnp.pad(value, ((0, padded), (0, 0)))
    for axis, bit in stages:
        value = halve(value, axis, bit)
    for axis, bit in stages[::-1]:
        value = double(value, axis, bit)
    return value[:rows] if padded else value


def rows_after(first_rows):
    tm, chan = lax.axis_size("tm"), lax.axis_size("chan")
    total = tm * chan
    return lax.ppermute(first_rows, ("tm", "chan"), [(i, i - 1) for i in range(1, total)])


def gram_kernel(lags_ref, rows_ref, after_ref, out_ref, ext_ref, high_ref, low_ref):
    rows = rows_ref.shape[0]
    lag_count = lags_ref.shape[0]
    width = NODES // 4
    ext_ref[:rows, :] = rows_ref[...]
    ext_ref[rows:, :] = after_ref[...]
    lane_part = lax.broadcasted_iota(jnp.int32, (BLOCK, BLOCK), 1) // width

    def build(step, _):
        start = step * BLOCK
        here = pl.ds(pl.multiple_of(start, BLOCK), BLOCK)
        for half in range(2):
            lagged = [ext_ref[pl.ds(start + lags_ref[4 * half + i], BLOCK), :] for i in range(4)]
            for group in range(4):
                block = None
                for i in range(4):
                    shift = (i - group) % 4 * width
                    part = pltpu.roll(lagged[i], shift, 1) if shift else lagged[i]
                    block = part if block is None else jnp.where(lane_part == i, part, block)
                high = block.astype(jnp.bfloat16)
                low = (block - high.astype(jnp.float32)).astype(jnp.bfloat16)
                column = (2 * group + half) * BLOCK
                high_ref[here, column : column + BLOCK] = high
                low_ref[here, column : column + BLOCK] = low
        return 0

    lax.fori_loop(0, rows // BLOCK, build, 0)
    count = lag_count * NODES // BLOCK

    def product(left, right):
        return lax.dot_general(left, right, CONTRACT_ROWS, preferred_element_type=jnp.float32)

    index = 0
    for k in range(count):
        mine = slice(k * BLOCK, (k + 1) * BLOCK)
        rest = slice(k * BLOCK, None)
        panel = product(high_ref[:, mine], high_ref[:, rest])
        panel = panel + product(high_ref[:, mine], low_ref[:, rest])
        panel = panel + product(low_ref[:, mine], high_ref[:, rest])
        for j in range(count - k):
            out_ref[index * BLOCK : (index + 1) * BLOCK, :] = panel[:, j * BLOCK : (j + 1) * BLOCK]
            index += 1


def gram_blocks(rows, after, lags):
    size = lags.shape[0] * NODES
    count = size // BLOCK
    blocks = count * (count + 1) // 2
    return pl.pallas_call(
        gram_kernel,
        out_shape=jax.ShapeDtypeStruct((blocks * BLOCK, BLOCK), jnp.float32),
        in_specs=[
            pl.BlockSpec(memory_space=pltpu.SMEM),
            pl.BlockSpec(memory_space=pltpu.VMEM),
            pl.BlockSpec(memory_space=pltpu.VMEM),
        ],
        out_specs=pl.BlockSpec(memory_space=pltpu.VMEM),
        scratch_shapes=[
            pltpu.VMEM((rows.shape[0] + after.shape[0], NODES), jnp.float32),
            pltpu.VMEM((rows.shape[0], size), jnp.bfloat16),
            pltpu.VMEM((rows.shape[0], size), jnp.bfloat16),
        ],
        compiler_params=pltpu.CompilerParams(vmem_limit_bytes=40 << 20),
    )(lags, rows, after)


def row_of(value, index):
    return jnp.broadcast_to(value[index : index + 1, :], value.shape)


def column_of(value, index):
    return jnp.broadcast_to(value[:, index : index + 1], value.shape)


def factor_block(block):
    count = len(block)
    sub = lax.broadcasted_iota(jnp.int32, (GROUP, BLOCK), 0)
    lane = lax.broadcasted_iota(jnp.int32, (GROUP, BLOCK), 1)
    block = list(block)
    inverse = [jnp.where(lane == sub + GROUP * s, 1.0, 0.0) for s in range(count)]
    for g in range(count):
        columns = [column_of(block[g], GROUP * g + m) for m in range(GROUP)]
        top, top_inverse = block[g], inverse[g]
        scale, factors, rows, inverse_rows = [], {}, [], []
        for m in range(GROUP):
            scale.append(lax.rsqrt(row_of(columns[m], m)))
            rows.append(row_of(top, m) * scale[m])
            inverse_rows.append(row_of(top_inverse, m) * scale[m])
            left = columns[m] * scale[m]
            for n in range(m + 1, GROUP):
                factors[m, n] = row_of(left, n)
                columns[n] = columns[n] - left * factors[m, n]
            below = jnp.where(sub > m, left, 0.0)
            top = jnp.where(sub == m, rows[m], top - below * rows[m])
            top_inverse = jnp.where(sub == m, inverse_rows[m], top_inverse - below * inverse_rows[m])
        block[g] = jnp.where(lane >= sub + GROUP * g, top, 0.0)
        inverse[g] = top_inverse
        for s in range(g + 1, count):
            columns = [column_of(block[s], GROUP * g + m) for m in range(GROUP)]
            for m in range(GROUP):
                left = columns[m] * scale[m]
                for n in range(m + 1, GROUP):
                    columns[n] = columns[n] - left * factors[m, n]
                block[s] = block[s] - left * rows[m]
                inverse[s] = inverse[s] - left * inverse_rows[m]
    return block, inverse


def cholesky_kernel(scale, blocks_ref, out_ref, panel_ref, inverse_ref):
    size = out_ref.shape[0]
    count = size // BLOCK
    first = [k * count - k * (k - 1) // 2 for k in range(count)]
    out_ref[...] = jnp.zeros_like(out_ref)

    def step(k, _):
        start = pl.multiple_of(k * BLOCK, BLOCK)
        for kk in range(count):

            @pl.when(k == kk)
            def _():
                mine = slice(kk * BLOCK, (kk + 1) * BLOCK)
                for j in range(kk, count):
                    place = (first[kk] + j - kk) * BLOCK
                    panel_ref[:, j * BLOCK : (j + 1) * BLOCK] = blocks_ref[place : place + BLOCK, :] * scale
                if kk:
                    panel_ref[:, kk * BLOCK :] -= lax.dot_general(
                        out_ref[: kk * BLOCK, mine],
                        out_ref[: kk * BLOCK, kk * BLOCK :],
                        CONTRACT_ROWS,
                        precision=HIGHEST,
                        preferred_element_type=jnp.float32,
                    )

        block = [panel_ref[GROUP * s : GROUP * (s + 1), pl.ds(start, BLOCK)] for s in range(BLOCK // GROUP)]
        block, inverse = factor_block(block)
        for s in range(BLOCK // GROUP):
            out_ref[pl.ds(pl.multiple_of(start + GROUP * s, GROUP), GROUP), pl.ds(start, BLOCK)] = block[s]
            inverse_ref[GROUP * s : GROUP * (s + 1), :] = inverse[s]
        for kk in range(count - 1):

            @pl.when(k == kk)
            def _():
                out_ref[kk * BLOCK : (kk + 1) * BLOCK, (kk + 1) * BLOCK :] = jnp.dot(
                    inverse_ref[...],
                    panel_ref[:, (kk + 1) * BLOCK :],
                    precision=HIGHEST,
                    preferred_element_type=jnp.float32,
                )

        return 0

    lax.fori_loop(0, count, step, 0)


def cholesky(blocks, size, scale):
    return pl.pallas_call(
        functools.partial(cholesky_kernel, scale),
        out_shape=jax.ShapeDtypeStruct((size, size), jnp.float32),
        in_specs=[pl.BlockSpec(memory_space=pltpu.VMEM)],
        out_specs=pl.BlockSpec(memory_space=pltpu.VMEM),
        scratch_shapes=[pltpu.VMEM((BLOCK, size), jnp.float32), pltpu.VMEM((BLOCK, BLOCK), jnp.float32)],
        compiler_params=pltpu.CompilerParams(vmem_limit_bytes=40 << 20),
    )(blocks)


def on_device(signals, channel_node, lag_offsets):
    node_scale = 1.0 / math.sqrt(CH // NODES)
    onehot = jnp.where(channel_node[:, None] == jnp.arange(NODES, dtype=jnp.int32)[None, :], node_scale, 0.0)
    nodes = jnp.dot(signals, onehot.astype(jnp.bfloat16), preferred_element_type=jnp.float32)
    total_rows = nodes.shape[0] * lax.axis_size("tm")
    nodes = scatter_rows(nodes, "chan")
    after = rows_after(nodes[:MAXLAG])
    blocks = gram_blocks(nodes, after, lag_offsets)
    blocks = sum_over_devices(blocks)
    return cholesky(blocks, lag_offsets.shape[0] * NODES, 1.0 / total_rows)


def solution(mesh):
    return jax.shard_map(
        on_device, mesh=mesh, in_specs=(P("tm", "chan"), P("chan"), P()), out_specs=P(), check_vma=False
    )
```

```python
import functools
import math

import jax
import jax.numpy as jnp
from jax import lax
from jax.experimental import pallas as pl
from jax.experimental.pallas import tpu as pltpu
from jax.sharding import PartitionSpec as P

NODES = 128
CH = 2048
MAXLAG = 512
BLOCK = 128
GROUP = 8
HIGHEST = lax.Precision.HIGHEST
CONTRACT_ROWS = (((0,), (0,)), ((), ()))


def swap(value, axis, bit):
    count = lax.axis_size(axis)
    return lax.ppermute(value, axis, [(i, i ^ bit) for i in range(count)])


def bits_of(axis):
    count = lax.axis_size(axis)
    return [1 << i for i in range(count.bit_length() - 1)]


def halve(value, axis, bit):
    half = value.shape[0] // 2
    mine = (lax.axis_index(axis) // bit) % 2
    send = lax.dynamic_slice_in_dim(value, (1 - mine) * half, half, 0)
    keep = lax.dynamic_slice_in_dim(value, mine * half, half, 0)
    return keep + swap(send, axis, bit)


def double(value, axis, bit):
    mine = (lax.axis_index(axis) // bit) % 2
    other = swap(value, axis, bit)
    low = jnp.where(mine == 0, value, other)
    high = jnp.where(mine == 0, other, value)
    return jnp.concatenate([low, high], axis=0)


def sum_over_time_blocks(value):
    for bit in bits_of("tm"):
        value = halve(value, "tm", bit)
    for bit in bits_of("tm")[::-1]:
        value = double(value, "tm", bit)
    return value


def first_rows_of_next(rows):
    count = lax.axis_size("tm")
    return lax.ppermute(rows, "tm", [(i, i - 1) for i in range(1, count)])


def project_kernel(half_ref, nodes_ref, signals_ref, out_ref, onehot_ref):
    @pl.when(pl.program_id(0) == 0)
    def _():
        node = lax.broadcasted_iota(jnp.int32, onehot_ref.shape, 0)
        scale = 1.0 / math.sqrt(CH // NODES)
        onehot_ref[...] = jnp.where(node == nodes_ref[...], scale, 0.0).astype(jnp.bfloat16)

    out_ref[...] = lax.dot_general(
        signals_ref[...], onehot_ref[...], (((1,), (1,)), ((), ())), preferred_element_type=jnp.float32
    )


def project(signals, channel_node, first, rows, half):
    channels = signals.shape[1]
    step = min(512, rows // 2)
    steps = rows // 2 // step
    grid_spec = pltpu.PrefetchScalarGridSpec(
        num_scalar_prefetch=1,
        grid=(steps,),
        in_specs=[
            pl.BlockSpec((1, channels), lambda i, half: (0, 0)),
            pl.BlockSpec((step, channels), lambda i, half: (first // step + half[0] * steps + i, 0)),
        ],
        out_specs=pl.BlockSpec((step, NODES), lambda i, half: (i, 0)),
        scratch_shapes=[pltpu.VMEM((NODES, channels), jnp.bfloat16)],
    )
    return pl.pallas_call(
        project_kernel,
        out_shape=jax.ShapeDtypeStruct((rows // 2, NODES), jnp.float32),
        grid_spec=grid_spec,
        cost_estimate=pl.CostEstimate(flops=rows * channels * NODES, bytes_accessed=rows * (channels + 2 * NODES), transcendentals=0),
    )(half, channel_node.reshape(1, channels), signals)


def gram_kernel(first, last, half_ref, lags_ref, *refs):
    refs = list(refs)
    mine_ref, other_ref = refs.pop(0), refs.pop(0)
    sum_in_ref, tail_in_ref = (None, None) if first else (refs.pop(0), refs.pop(0))
    after_ref = refs.pop(0) if last else None
    out_ref = refs.pop(0)
    tail_out_ref = None if last else refs.pop(0)
    ext_ref, high_ref, low_ref, sum_ref = refs
    half = mine_ref.shape[0]
    lead = 0 if first else MAXLAG
    lag_count = lags_ref.shape[0]
    step_rows = high_ref.shape[0]
    own = pl.multiple_of(lead + half_ref[0] * half, math.gcd(lead, half))
    others = pl.multiple_of(lead + (1 - half_ref[0]) * half, math.gcd(lead, half))
    ext_ref[pl.ds(own, half), :] = mine_ref[...]
    ext_ref[pl.ds(others, half), :] = other_ref[...]
    end = lead + 2 * half
    if not first:
        ext_ref[:lead, :] = tail_in_ref[...]
    if last:
        ext_ref[end:, :] = after_ref[...]
    else:
        tail_out_ref[...] = ext_ref[end - MAXLAG : end, :]
    steps = (end if last else end - MAXLAG) // step_rows
    sum_ref[...] = jnp.zeros_like(sum_ref) if first else sum_in_ref[...]
    part = 128

    def step(i, _):
        start = i * step_rows
        for lag in range(lag_count):
            for row in range(0, step_rows, part):
                value = ext_ref[pl.ds(start + row + lags_ref[lag], part), :]
                high = value.astype(jnp.bfloat16)
                high_ref[row : row + part, lag * NODES : (lag + 1) * NODES] = high
                low_ref[row : row + part, lag * NODES : (lag + 1) * NODES] = (
                    value - high.astype(jnp.float32)
                ).astype(jnp.bfloat16)

        def product(left, right):
            return lax.dot_general(left, right, CONTRACT_ROWS, preferred_element_type=jnp.float32)

        left = slice(0, 2 * NODES)
        total = product(high_ref[:, left], high_ref[...])
        total = total + product(high_ref[:, left], low_ref[...])
        total = total + product(low_ref[:, left], high_ref[...])
        sum_ref[...] += total
        return 0

    lax.fori_loop(0, steps, step, 0)
    if last:
        far = lag_count - 2
        for j in range(far):
            out_ref[j * NODES : (j + 1) * NODES, :] = sum_ref[:NODES, j * NODES : (j + 1) * NODES]
            place = (far + j) * NODES
            out_ref[place : place + NODES, :] = sum_ref[NODES:, (j + 1) * NODES : (j + 2) * NODES]
        which = half_ref[1]
        row = pl.multiple_of(which * NODES, NODES)
        column = pl.multiple_of((far + which) * NODES, NODES)
        out_ref[2 * far * NODES :, :] = sum_ref[pl.ds(row, NODES), pl.ds(column, NODES)]
    else:
        out_ref[...] = sum_ref[...]


def gram_part(half, lags, mine, other, carried, after):
    first, last = carried is None, after is not None
    count = lags.shape[0]
    blocks = 2 * (count - 2) + 1
    operands = [half, lags, mine, other]
    if not first:
        operands += list(carried)
    if last:
        operands.append(after)
    if last:
        out_shape = jax.ShapeDtypeStruct((blocks * NODES, NODES), jnp.float32)
    else:
        out_shape = (
            jax.ShapeDtypeStruct((2 * NODES, count * NODES), jnp.float32),
            jax.ShapeDtypeStruct((MAXLAG, NODES), jnp.float32),
        )
    rows = 2 * mine.shape[0] + (0 if first else MAXLAG) + (MAXLAG if last else 0)
    vmem = pl.BlockSpec(memory_space=pltpu.VMEM)
    smem = pl.BlockSpec(memory_space=pltpu.SMEM)
    step_rows = 512
    return pl.pallas_call(
        functools.partial(gram_kernel, first, last),
        out_shape=out_shape,
        in_specs=[smem, smem] + [vmem] * (len(operands) - 2),
        out_specs=vmem if last else (vmem, vmem),
        scratch_shapes=[
            pltpu.VMEM((rows, NODES), jnp.float32),
            pltpu.VMEM((step_rows, count * NODES), jnp.bfloat16),
            pltpu.VMEM((step_rows, count * NODES), jnp.bfloat16),
            pltpu.VMEM((2 * NODES, count * NODES), jnp.float32),
        ],
        compiler_params=pltpu.CompilerParams(vmem_limit_bytes=40 << 20),
        cost_estimate=pl.CostEstimate(flops=rows * NODES * NODES * count * 12, bytes_accessed=rows * NODES * 4, transcendentals=0),
    )(*operands)


def row_of(value, index):
    return jnp.broadcast_to(value[index : index + 1, :], value.shape)


def column_of(value, index):
    return jnp.broadcast_to(value[:, index : index + 1], value.shape)


def factor_block(block):
    count = len(block)
    sub = lax.broadcasted_iota(jnp.int32, (GROUP, BLOCK), 0)
    lane = lax.broadcasted_iota(jnp.int32, (GROUP, BLOCK), 1)
    block = list(block)
    inverse = [jnp.where(lane == sub + GROUP * s, 1.0, 0.0) for s in range(count)]
    for g in range(count):
        columns = [column_of(block[g], GROUP * g + m) for m in range(GROUP)]
        top, top_inverse = block[g], inverse[g]
        scale, factors, rows, inverse_rows = [], {}, [], []
        for m in range(GROUP):
            scale.append(lax.rsqrt(row_of(columns[m], m)))
            rows.append(row_of(top, m) * scale[m])
            inverse_rows.append(row_of(top_inverse, m) * scale[m])
            left = columns[m] * scale[m]
            for n in range(m + 1, GROUP):
                factors[m, n] = row_of(left, n)
                columns[n] = columns[n] - left * factors[m, n]
            below = jnp.where(sub > m, left, 0.0)
            top = jnp.where(sub == m, rows[m], top - below * rows[m])
            top_inverse = jnp.where(sub == m, inverse_rows[m], top_inverse - below * inverse_rows[m])
        block[g] = jnp.where(lane >= sub + GROUP * g, top, 0.0)
        inverse[g] = top_inverse
        for s in range(g + 1, count):
            columns = [column_of(block[s], GROUP * g + m) for m in range(GROUP)]
            for m in range(GROUP):
                left = columns[m] * scale[m]
                for n in range(m + 1, GROUP):
                    columns[n] = columns[n] - left * factors[m, n]
                block[s] = block[s] - left * rows[m]
                inverse[s] = inverse[s] - left * inverse_rows[m]
    return block, inverse


def arrange(half_ref, mine_ref, other_ref, natural_ref, ordered_ref):
    chan_count = 4
    lag_count = 2 * chan_count
    far = lag_count // 2
    width = NODES // chan_count
    each = (2 * far + 1) * NODES

    def place(ref, low):
        for high in range(2):
            chan = 2 * high + low
            pairs = [(2 * chan + i, (2 * chan + i + d) % lag_count) for i in range(2) for d in range(far)]
            odd = 2 * chan // far
            pairs.append((2 * chan + odd, (2 * chan + odd + far) % lag_count))
            for index, (left, right) in enumerate(pairs):
                start = high * each + index * NODES
                block = ref[start : start + NODES, :]
                natural_ref[left * NODES : (left + 1) * NODES, right * NODES : (right + 1) * NODES] = block
                if left != right:
                    natural_ref[right * NODES : (right + 1) * NODES, left * NODES : (left + 1) * NODES] = block.T

    for low in range(2):

        @pl.when(half_ref[0] == low)
        def _():
            place(mine_ref, low)
            place(other_ref, 1 - low)

    lane_part = lax.broadcasted_iota(jnp.int32, (width, NODES), 1) // width

    def rows_of_lag(lag, _):
        for group in range(chan_count):
            source = pl.ds(pl.multiple_of(lag * NODES + group * width, width), width)
            target = pl.ds(pl.multiple_of(group * lag_count * width + lag * width, width), width)
            for half in range(2):
                parts = [natural_ref[source, (4 * half + i) * NODES : (4 * half + i + 1) * NODES] for i in range(4)]
                for other in range(group, chan_count):
                    block = None
                    for i in range(4):
                        shift = (i - other) % 4 * width
                        part = pltpu.roll(parts[i], shift, 1) if shift else parts[i]
                        block = part if block is None else jnp.where(lane_part == i, part, block)
                    column = (2 * other + half) * BLOCK
                    ordered_ref[target, column : column + BLOCK] = block
        return 0

    lax.fori_loop(0, lag_count, rows_of_lag, 0)


def cholesky_kernel(scale, half_ref, mine_ref, other_ref, out_ref, natural_ref, ordered_ref, panel_ref, inverse_ref):
    arrange(half_ref, mine_ref, other_ref, natural_ref, ordered_ref)
    size = out_ref.shape[0]
    count = size // BLOCK
    out_ref[...] = jnp.zeros_like(out_ref)

    def step(k, _):
        start = pl.multiple_of(k * BLOCK, BLOCK)
        for kk in range(count):

            @pl.when(k == kk)
            def _():
                mine = slice(kk * BLOCK, (kk + 1) * BLOCK)
                panel = ordered_ref[mine, kk * BLOCK :] * scale
                if kk:
                    panel = panel - lax.dot_general(
                        out_ref[: kk * BLOCK, mine],
                        out_ref[: kk * BLOCK, kk * BLOCK :],
                        CONTRACT_ROWS,
                        precision=HIGHEST,
                        preferred_element_type=jnp.float32,
                    )
                panel_ref[:, kk * BLOCK :] = panel

        block = [panel_ref[GROUP * s : GROUP * (s + 1), pl.ds(start, BLOCK)] for s in range(BLOCK // GROUP)]
        block, inverse = factor_block(block)
        for s in range(BLOCK // GROUP):
            out_ref[pl.ds(pl.multiple_of(start + GROUP * s, GROUP), GROUP), pl.ds(start, BLOCK)] = block[s]
            inverse_ref[GROUP * s : GROUP * (s + 1), :] = inverse[s]
        for kk in range(count - 1):

            @pl.when(k == kk)
            def _():
                out_ref[kk * BLOCK : (kk + 1) * BLOCK, (kk + 1) * BLOCK :] = jnp.dot(
                    inverse_ref[...],
                    panel_ref[:, (kk + 1) * BLOCK :],
                    precision=HIGHEST,
                    preferred_element_type=jnp.float32,
                )

        return 0

    lax.fori_loop(0, count, step, 0)


def cholesky(half, mine, other, size, scale):
    vmem = pl.BlockSpec(memory_space=pltpu.VMEM)
    return pl.pallas_call(
        functools.partial(cholesky_kernel, scale),
        out_shape=jax.ShapeDtypeStruct((size, size), jnp.float32),
        in_specs=[pl.BlockSpec(memory_space=pltpu.SMEM), vmem, vmem],
        out_specs=vmem,
        scratch_shapes=[
            pltpu.VMEM((size, size), jnp.float32),
            pltpu.VMEM((size, size), jnp.float32),
            pltpu.VMEM((BLOCK, size), jnp.float32),
            pltpu.VMEM((BLOCK, BLOCK), jnp.float32),
        ],
        compiler_params=pltpu.CompilerParams(vmem_limit_bytes=48 << 20),
    )(half, mine, other)


CHUNKS = 2


def on_device(signals, channel_node, lag_offsets):
    rows = signals.shape[0]
    lag_count = lag_offsets.shape[0]
    chan = lax.axis_index("chan")
    half = jnp.stack([chan % 2, 4 * chan // lag_count])
    span = lag_count // 2 + 2
    lags = lag_offsets[(2 * chan + jnp.arange(span, dtype=jnp.int32)) % lag_count]
    size = rows // CHUNKS
    carried = after = None
    for index in range(CHUNKS):
        first, last = index == 0, index == CHUNKS - 1
        send = project(signals, channel_node, index * size, size, 1 - half)
        received = swap(send, "chan", 1)
        keep = project(signals, channel_node, index * size, size, half)
        value = keep + received
        value = value + swap(value, "chan", 2)
        other = swap(value, "chan", 1)
        if first:
            head = jnp.where(half[0] == 0, value[:MAXLAG], other[:MAXLAG])
            after = first_rows_of_next(head)
        carried = gram_part(half, lags, value, other, carried, after if last else None)
    blocks = sum_over_time_blocks(carried)
    blocks = double(blocks, "chan", 2)
    other = swap(blocks, "chan", 1)
    return cholesky(half, blocks, other, lag_count * NODES, 1.0 / (rows * lax.axis_size("tm")))


def solution(mesh):
    return jax.shard_map(
        on_device, mesh=mesh, in_specs=(P("tm", "chan"), P("chan"), P()), out_specs=P(), check_vma=False
    )
```

```python
import functools
import math

import jax
import jax.numpy as jnp
from jax import lax
from jax.experimental import pallas as pl
from jax.experimental.pallas import tpu as pltpu
from jax.sharding import PartitionSpec as P

NODES = 128
CH = 2048
MAXLAG = 512
BLOCK = 128
GROUP = 8
SPAN = 4
HIGHEST = lax.Precision.HIGHEST
CONTRACT_ROWS = (((0,), (0,)), ((), ()))


def swap(value, axis, bit):
    count = lax.axis_size(axis)
    return lax.ppermute(value, axis, [(i, i ^ bit) for i in range(count)])


def bits_of(axis):
    count = lax.axis_size(axis)
    return [1 << i for i in range(count.bit_length() - 1)]


def halve(value, axis, bit):
    half = value.shape[0] // 2
    mine = (lax.axis_index(axis) // bit) % 2
    send = lax.dynamic_slice_in_dim(value, (1 - mine) * half, half, 0)
    keep = lax.dynamic_slice_in_dim(value, mine * half, half, 0)
    return keep + swap(send, axis, bit)


def double(value, axis, bit):
    mine = (lax.axis_index(axis) // bit) % 2
    other = swap(value, axis, bit)
    low = jnp.where(mine == 0, value, other)
    high = jnp.where(mine == 0, other, value)
    return jnp.concatenate([low, high], axis=0)


def sum_over_time_blocks(value):
    for bit in bits_of("tm"):
        value = halve(value, "tm", bit)
    for bit in bits_of("tm")[::-1]:
        value = double(value, "tm", bit)
    return value


def add_kernel(left_ref, right_ref, *refs):
    refs[-1][...] = left_ref[...] + right_ref[...]


def add(left, right, *earlier):
    vmem = pl.BlockSpec(memory_space=pltpu.VMEM)
    return pl.pallas_call(
        add_kernel,
        out_shape=jax.ShapeDtypeStruct(left.shape, left.dtype),
        in_specs=[vmem, vmem] + [pl.BlockSpec(memory_space=pl.ANY)] * len(earlier),
        out_specs=vmem,
    )(left, right, *earlier)


def first_rows_of_next(rows):
    count = lax.axis_size("tm")
    return lax.ppermute(rows, "tm", [(i, i - 1) for i in range(1, count)])


def project_kernel(half_ref, nodes_ref, signals_ref, out_ref, onehot_ref):
    @pl.when(pl.program_id(0) == 0)
    def _():
        node = lax.broadcasted_iota(jnp.int32, onehot_ref.shape, 0)
        scale = 1.0 / math.sqrt(CH // NODES)
        onehot_ref[...] = jnp.where(node == nodes_ref[...], scale, 0.0).astype(jnp.bfloat16)

    out_ref[...] = lax.dot_general(
        signals_ref[...], onehot_ref[...], (((1,), (1,)), ((), ())), preferred_element_type=jnp.float32
    )


def project(signals, channel_node, first, rows, half):
    channels = signals.shape[1]
    step = min(512, rows // 2)
    steps = rows // 2 // step
    grid_spec = pltpu.PrefetchScalarGridSpec(
        num_scalar_prefetch=1,
        grid=(steps,),
        in_specs=[
            pl.BlockSpec((1, channels), lambda i, half: (0, 0)),
            pl.BlockSpec((step, channels), lambda i, half: (first // step + half[0] * steps + i, 0)),
        ],
        out_specs=pl.BlockSpec((step, NODES), lambda i, half: (i, 0)),
        scratch_shapes=[pltpu.VMEM((NODES, channels), jnp.bfloat16)],
    )
    return pl.pallas_call(
        project_kernel,
        out_shape=jax.ShapeDtypeStruct((rows // 2, NODES), jnp.float32),
        grid_spec=grid_spec,
        cost_estimate=pl.CostEstimate(flops=rows * channels * NODES, bytes_accessed=rows * (channels + 2 * NODES), transcendentals=0),
    )(half, channel_node.reshape(1, channels), signals)


def gram_kernel(first, last, earlier, half_ref, lags_ref, *refs):
    refs = list(refs)
    mine_ref, other_ref = refs.pop(0), refs.pop(0)
    sum_in_ref, tail_in_ref = (None, None) if first else (refs.pop(0), refs.pop(0))
    after_ref = refs.pop(0) if last else None
    del refs[:earlier]
    out_ref = refs.pop(0)
    tail_out_ref = None if last else refs.pop(0)
    ext_ref, high_ref, low_ref, sum_ref = refs
    half = mine_ref.shape[0]
    lead = 0 if first else MAXLAG
    lag_count = lags_ref.shape[0]
    step_rows = high_ref.shape[0]
    own = pl.multiple_of(lead + half_ref[0] * half, math.gcd(lead, half))
    others = pl.multiple_of(lead + (1 - half_ref[0]) * half, math.gcd(lead, half))
    ext_ref[pl.ds(own, half), :] = mine_ref[...]
    ext_ref[pl.ds(others, half), :] = other_ref[...]
    end = lead + 2 * half
    if not first:
        ext_ref[:lead, :] = tail_in_ref[...]
    if last:
        ext_ref[end:, :] = after_ref[...]
    else:
        tail_out_ref[...] = ext_ref[end - MAXLAG : end, :]
    steps = (end if last else end - MAXLAG) // step_rows
    sum_ref[...] = jnp.zeros_like(sum_ref) if first else sum_in_ref[...]
    part = 128

    def step(i, _):
        start = i * step_rows
        for lag in range(lag_count):
            for row in range(0, step_rows, part):
                value = ext_ref[pl.ds(start + row + lags_ref[lag], part), :]
                high = value.astype(jnp.bfloat16)
                high_ref[row : row + part, lag * NODES : (lag + 1) * NODES] = high
                low_ref[row : row + part, lag * NODES : (lag + 1) * NODES] = (
                    value - high.astype(jnp.float32)
                ).astype(jnp.bfloat16)

        def product(left, right):
            return lax.dot_general(left, right, CONTRACT_ROWS, preferred_element_type=jnp.float32)

        left = slice(0, 2 * NODES)
        total = product(high_ref[:, left], high_ref[...])
        total = total + product(high_ref[:, left], low_ref[...])
        total = total + product(low_ref[:, left], high_ref[...])
        sum_ref[...] += total
        return 0

    lax.fori_loop(0, steps, step, 0)
    if last:
        far = lag_count - 2
        for j in range(far):
            out_ref[j * NODES : (j + 1) * NODES, :] = sum_ref[:NODES, j * NODES : (j + 1) * NODES]
            place = (far + j) * NODES
            out_ref[place : place + NODES, :] = sum_ref[NODES:, (j + 1) * NODES : (j + 2) * NODES]
        which = half_ref[1]
        row = pl.multiple_of(which * NODES, NODES)
        column = pl.multiple_of((far + which) * NODES, NODES)
        out_ref[2 * far * NODES :, :] = sum_ref[pl.ds(row, NODES), pl.ds(column, NODES)]
    else:
        out_ref[...] = sum_ref[...]


def gram_part(half, lags, mine, other, carried, after, earlier):
    first, last = carried is None, after is not None
    count = lags.shape[0]
    blocks = 2 * (count - 2) + 1
    operands = [half, lags, mine, other]
    if not first:
        operands += list(carried)
    if last:
        operands.append(after)
    if last:
        out_shape = jax.ShapeDtypeStruct((blocks * NODES, NODES), jnp.float32)
    else:
        out_shape = (
            jax.ShapeDtypeStruct((2 * NODES, count * NODES), jnp.float32),
            jax.ShapeDtypeStruct((MAXLAG, NODES), jnp.float32),
        )
    rows = 2 * mine.shape[0] + (0 if first else MAXLAG) + (MAXLAG if last else 0)
    vmem = pl.BlockSpec(memory_space=pltpu.VMEM)
    smem = pl.BlockSpec(memory_space=pltpu.SMEM)
    step_rows = 512
    return pl.pallas_call(
        functools.partial(gram_kernel, first, last, len(earlier)),
        out_shape=out_shape,
        in_specs=[smem, smem] + [vmem] * (len(operands) - 2) + [pl.BlockSpec(memory_space=pl.ANY)] * len(earlier),
        out_specs=vmem if last else (vmem, vmem),
        scratch_shapes=[
            pltpu.VMEM((rows, NODES), jnp.float32),
            pltpu.VMEM((step_rows, count * NODES), jnp.bfloat16),
            pltpu.VMEM((step_rows, count * NODES), jnp.bfloat16),
            pltpu.VMEM((2 * NODES, count * NODES), jnp.float32),
        ],
        compiler_params=pltpu.CompilerParams(vmem_limit_bytes=40 << 20),
        cost_estimate=pl.CostEstimate(flops=rows * NODES * NODES * count * 12, bytes_accessed=rows * NODES * 4, transcendentals=0),
    )(*operands, *earlier)


def row_of(value, index):
    return jnp.broadcast_to(value[index : index + 1, :], value.shape)


def column_of(value, index):
    return jnp.broadcast_to(value[:, index : index + 1], value.shape)


def factor_block(block):
    count = len(block)
    sub = lax.broadcasted_iota(jnp.int32, (GROUP, BLOCK), 0)
    lane = lax.broadcasted_iota(jnp.int32, (GROUP, BLOCK), 1)
    state = list(block)
    result = [None] * count
    full = [None] * count
    columns = [column_of(state[0], m) for m in range(GROUP)]
    for g in range(count):
        first_lane, next_lane = GROUP * g, GROUP * (g + 1)
        here = (lane >= first_lane) & (lane < next_lane)
        span = g // SPAN
        more = g + 1 < count
        if more:
            next_columns = [column_of(state[g + 1], next_lane + m) for m in range(GROUP)]
            next_left = [column_of(state[g + 1], first_lane + m) for m in range(GROUP)]
            state[g + 1] = jnp.where(here, 0.0, state[g + 1])
        top = jnp.where(here, jnp.where(lane == sub + first_lane, 1.0, 0.0), state[g])
        diagonal = jnp.zeros_like(top)
        scale, factors, rows = [], {}, []
        for m in range(GROUP):
            pivot = row_of(columns[m], m)
            scale.append(lax.rsqrt(pivot))
            left = columns[m] * scale[m]
            for n in range(m + 1, GROUP):
                factors[m, n] = row_of(left, n)
                columns[n] = columns[n] - left * factors[m, n]
            if more:
                next_left[m] = next_left[m] * scale[m]
                for n in range(m + 1, GROUP):
                    next_left[n] = next_left[n] - next_left[m] * factors[m, n]
                for n in range(GROUP):
                    next_columns[n] = next_columns[n] - next_left[m] * row_of(next_left[m], n)
            rows.append(row_of(top, m) * scale[m])
            below = jnp.where(sub > m, left, 0.0)
            top = jnp.where(sub == m, rows[m], top - below * rows[m])
            entries = pivot * scale[m]
            for n in range(m + 1, GROUP):
                entries = jnp.where(lane == first_lane + n, factors[m, n], entries)
            diagonal = jnp.where(sub == m, entries, diagonal)
            if more:
                state[g + 1] = state[g + 1] - next_left[m] * rows[m]
        full[g] = top
        result[g] = jnp.where(lane >= next_lane, top, jnp.where(lane >= sub + first_lane, diagonal, 0.0))
        state[g] = jnp.where(lane < next_lane, top, 0.0)
        columns = next_columns
        for s in range(g + 2, min(count, (span + 2) * SPAN)):
            left = [column_of(state[s], first_lane + m) for m in range(GROUP)]
            value = jnp.where(here, 0.0, state[s])
            for m in range(GROUP):
                left[m] = left[m] * scale[m]
                for n in range(m + 1, GROUP):
                    left[n] = left[n] - left[m] * factors[m, n]
                value = value - left[m] * rows[m]
            state[s] = value
        rest = (span + 2) * SPAN
        if g % SPAN == SPAN - 1 and rest < count:
            begin = span * SPAN
            left = jnp.concatenate(full[begin : g + 1], axis=0)
            right = [
                jnp.where((lane >= GROUP * (i + 1)) & (lane < next_lane), 0.0, full[i]) for i in range(begin, g + 1)
            ]
            update = lax.dot_general(
                left[:, GROUP * rest :],
                jnp.concatenate(right, axis=0),
                CONTRACT_ROWS,
                precision=HIGHEST,
                preferred_element_type=jnp.float32,
            )
            inside = (lane >= GROUP * begin) & (lane < next_lane)
            for s in range(rest, count):
                place = GROUP * (s - rest)
                state[s] = jnp.where(inside, 0.0, state[s]) - update[place : place + GROUP]
    return result, state


def arrange(half_ref, mine_ref, other_ref, natural_ref, ordered_ref):
    chan_count = 4
    lag_count = 2 * chan_count
    far = lag_count // 2
    width = NODES // chan_count
    each = (2 * far + 1) * NODES

    def place(ref, low):
        for high in range(2):
            chan = 2 * high + low
            pairs = [(2 * chan + i, (2 * chan + i + d) % lag_count) for i in range(2) for d in range(far)]
            odd = 2 * chan // far
            pairs.append((2 * chan + odd, (2 * chan + odd + far) % lag_count))
            for index, (left, right) in enumerate(pairs):
                start = high * each + index * NODES
                block = ref[start : start + NODES, :]
                natural_ref[left * NODES : (left + 1) * NODES, right * NODES : (right + 1) * NODES] = block
                if left != right:
                    natural_ref[right * NODES : (right + 1) * NODES, left * NODES : (left + 1) * NODES] = block.T

    for low in range(2):

        @pl.when(half_ref[0] == low)
        def _():
            place(mine_ref, low)
            place(other_ref, 1 - low)

    lane_part = lax.broadcasted_iota(jnp.int32, (width, NODES), 1) // width

    def rows_of_lag(lag, _):
        for group in range(chan_count):
            source = pl.ds(pl.multiple_of(lag * NODES + group * width, width), width)
            target = pl.ds(pl.multiple_of(group * lag_count * width + lag * width, width), width)
            for half in range(2):
                parts = [natural_ref[source, (4 * half + i) * NODES : (4 * half + i + 1) * NODES] for i in range(4)]
                for other in range(group, chan_count):
                    block = None
                    for i in range(4):
                        shift = (i - other) % 4 * width
                        part = pltpu.roll(parts[i], shift, 1) if shift else parts[i]
                        block = part if block is None else jnp.where(lane_part == i, part, block)
                    column = (2 * other + half) * BLOCK
                    ordered_ref[target, column : column + BLOCK] = block
        return 0

    lax.fori_loop(0, lag_count, rows_of_lag, 0)


def cholesky_kernel(scale, half_ref, mine_ref, other_ref, out_ref, natural_ref, ordered_ref, panel_ref, inverse_ref):
    arrange(half_ref, mine_ref, other_ref, natural_ref, ordered_ref)
    size = out_ref.shape[0]
    count = size // BLOCK
    out_ref[...] = jnp.zeros_like(out_ref)

    def step(k, _):
        start = pl.multiple_of(k * BLOCK, BLOCK)
        for kk in range(count):

            @pl.when(k == kk)
            def _():
                mine = slice(kk * BLOCK, (kk + 1) * BLOCK)
                panel = ordered_ref[mine, kk * BLOCK :] * scale
                if kk:
                    panel = panel - lax.dot_general(
                        out_ref[: kk * BLOCK, mine],
                        out_ref[: kk * BLOCK, kk * BLOCK :],
                        CONTRACT_ROWS,
                        precision=HIGHEST,
                        preferred_element_type=jnp.float32,
                    )
                panel_ref[:, kk * BLOCK :] = panel

        block = [panel_ref[GROUP * s : GROUP * (s + 1), pl.ds(start, BLOCK)] for s in range(BLOCK // GROUP)]
        block, inverse = factor_block(block)
        for s in range(BLOCK // GROUP):
            out_ref[pl.ds(pl.multiple_of(start + GROUP * s, GROUP), GROUP), pl.ds(start, BLOCK)] = block[s]
            inverse_ref[GROUP * s : GROUP * (s + 1), :] = inverse[s]
        for kk in range(count - 1):

            @pl.when(k == kk)
            def _():
                out_ref[kk * BLOCK : (kk + 1) * BLOCK, (kk + 1) * BLOCK :] = jnp.dot(
                    inverse_ref[...],
                    panel_ref[:, (kk + 1) * BLOCK :],
                    precision=HIGHEST,
                    preferred_element_type=jnp.float32,
                )

        return 0

    lax.fori_loop(0, count, step, 0)


def cholesky(half, mine, other, size, scale):
    vmem = pl.BlockSpec(memory_space=pltpu.VMEM)
    return pl.pallas_call(
        functools.partial(cholesky_kernel, scale),
        out_shape=jax.ShapeDtypeStruct((size, size), jnp.float32),
        in_specs=[pl.BlockSpec(memory_space=pltpu.SMEM), vmem, vmem],
        out_specs=vmem,
        scratch_shapes=[
            pltpu.VMEM((size, size), jnp.float32),
            pltpu.VMEM((size, size), jnp.float32),
            pltpu.VMEM((BLOCK, size), jnp.float32),
            pltpu.VMEM((BLOCK, BLOCK), jnp.float32),
        ],
        compiler_params=pltpu.CompilerParams(vmem_limit_bytes=48 << 20),
    )(half, mine, other)


CHUNKS = 2


def on_device(signals, channel_node, lag_offsets):
    rows = signals.shape[0]
    lag_count = lag_offsets.shape[0]
    chan = lax.axis_index("chan")
    half = jnp.stack([chan % 2, 4 * chan // lag_count])
    span = lag_count // 2 + 2
    lags = lag_offsets[(2 * chan + jnp.arange(span, dtype=jnp.int32)) % lag_count]
    size = rows // CHUNKS
    totals, sent = [], []
    for index in range(CHUNKS):
        send = project(signals, channel_node, index * size, size, 1 - half)
        received = swap(send, "chan", 1)
        keep = project(signals, channel_node, index * size, size, half)
        totals.append(keep + received)
        sent.append(swap(totals[-1], "chan", 2))
    carried = after = None
    for index in range(CHUNKS):
        first, last = index == 0, index == CHUNKS - 1
        value = add(totals[index], sent[index], *(totals[1:] if first else (carried[1],)))
        other = swap(value, "chan", 1)
        if first:
            head = jnp.where(half[0] == 0, value[:MAXLAG], other[:MAXLAG])
            after = first_rows_of_next(head)
        earlier = (head,) if first else ()
        carried = gram_part(half, lags, value, other, carried, after if last else None, earlier)
    blocks = sum_over_time_blocks(carried)
    blocks = double(blocks, "chan", 2)
    other = swap(blocks, "chan", 1)
    return cholesky(half, blocks, other, lag_count * NODES, 1.0 / (rows * lax.axis_size("tm")))


def solution(mesh):
    return jax.shard_map(
        on_device, mesh=mesh, in_specs=(P("tm", "chan"), P("chan"), P()), out_specs=P(), check_vma=False
    )
```

```python
import functools
import math

import jax
import jax.numpy as jnp
from jax import lax
from jax.experimental import pallas as pl
from jax.experimental.pallas import tpu as pltpu
from jax.sharding import PartitionSpec as P

NODES = 128
CH = 2048
MAXLAG = 512
BLOCK = 128
GROUP = 8
SPAN = 4
CHUNKS = 2
HIGHEST = lax.Precision.HIGHEST
CONTRACT_ROWS = (((0,), (0,)), ((), ()))


def swap(value, axis, bit):
    count = lax.axis_size(axis)
    return lax.ppermute(value, axis, [(i, i ^ bit) for i in range(count)])


def bits_of(axis):
    count = lax.axis_size(axis)
    return [1 << i for i in range(count.bit_length() - 1)]


def halve(value, axis, bit):
    half = value.shape[0] // 2
    mine = (lax.axis_index(axis) // bit) % 2
    send = lax.dynamic_slice_in_dim(value, (1 - mine) * half, half, 0)
    keep = lax.dynamic_slice_in_dim(value, mine * half, half, 0)
    return keep + swap(send, axis, bit)


def double(value, axis, bit):
    mine = (lax.axis_index(axis) // bit) % 2
    other = swap(value, axis, bit)
    low = jnp.where(mine == 0, value, other)
    high = jnp.where(mine == 0, other, value)
    return jnp.concatenate([low, high], axis=0)


def sum_over_time_blocks(value):
    for bit in bits_of("tm"):
        value = halve(value, "tm", bit)
    for bit in bits_of("tm")[::-1]:
        value = double(value, "tm", bit)
    return value


def add_kernel(left_ref, right_ref, *refs):
    refs[-1][...] = left_ref[...] + right_ref[...]


def add(left, right, *earlier):
    vmem = pl.BlockSpec(memory_space=pltpu.VMEM)
    return pl.pallas_call(
        add_kernel,
        out_shape=jax.ShapeDtypeStruct(left.shape, left.dtype),
        in_specs=[vmem, vmem] + [pl.BlockSpec(memory_space=pl.ANY)] * len(earlier),
        out_specs=vmem,
    )(left, right, *earlier)


def add_parts_kernel(left_ref, right_ref, *out_refs):
    start = 0
    for out_ref in out_refs:
        here = slice(start, start + out_ref.shape[0])
        out_ref[...] = left_ref[here, :] + right_ref[here, :]
        start += out_ref.shape[0]


def add_parts(left, right, parts):
    vmem = pl.BlockSpec(memory_space=pltpu.VMEM)
    part = jax.ShapeDtypeStruct((left.shape[0] // parts, left.shape[1]), left.dtype)
    return pl.pallas_call(
        add_parts_kernel,
        out_shape=(part,) * parts,
        in_specs=[vmem, vmem],
        out_specs=(vmem,) * parts,
    )(left, right)


def first_rows_of_next(rows):
    count = lax.axis_size("tm")
    return lax.ppermute(rows, "tm", [(i, i - 1) for i in range(1, count)])


def project_kernel(half_ref, nodes_ref, signals_ref, out_ref, onehot_ref):
    @pl.when(pl.program_id(0) == 0)
    def _():
        node = lax.broadcasted_iota(jnp.int32, onehot_ref.shape, 0)
        scale = 1.0 / math.sqrt(CH // NODES)
        onehot_ref[...] = jnp.where(node == nodes_ref[...], scale, 0.0).astype(jnp.bfloat16)

    out_ref[...] = lax.dot_general(
        signals_ref[...], onehot_ref[...], (((1,), (1,)), ((), ())), preferred_element_type=jnp.float32
    )


def project(signals, channel_node, half):
    rows, channels = signals.shape
    part = rows // CHUNKS // 2
    step = min(512, part)
    steps = part // step
    grid_spec = pltpu.PrefetchScalarGridSpec(
        num_scalar_prefetch=1,
        grid=(CHUNKS * steps,),
        in_specs=[
            pl.BlockSpec((1, channels), lambda i, half: (0, 0)),
            pl.BlockSpec((step, channels), lambda i, half: ((i // steps * 2 + half[0]) * steps + i % steps, 0)),
        ],
        out_specs=pl.BlockSpec((step, NODES), lambda i, half: (i, 0)),
        scratch_shapes=[pltpu.VMEM((NODES, channels), jnp.bfloat16)],
    )
    return pl.pallas_call(
        project_kernel,
        out_shape=jax.ShapeDtypeStruct((rows // 2, NODES), jnp.float32),
        grid_spec=grid_spec,
    )(half, channel_node.reshape(1, channels), signals)


def gram_kernel(first, last, earlier, chan_ref, all_lags_ref, *refs):
    refs = list(refs)
    mine_ref, other_ref = refs.pop(0), refs.pop(0)
    sum_in_ref, tail_in_ref = (None, None) if first else (refs.pop(0), refs.pop(0))
    after_ref = refs.pop(0) if last else None
    del refs[:earlier]
    out_ref = refs.pop(0)
    tail_out_ref = None if last else refs.pop(0)
    ext_ref, high_ref, low_ref, sum_ref = refs
    half = mine_ref.shape[0]
    lead = 0 if first else MAXLAG
    total_lags = all_lags_ref.shape[0]
    lag_count = sum_ref.shape[1] // NODES
    lags = [all_lags_ref[lax.rem(2 * chan_ref[0] + i, total_lags)] for i in range(lag_count)]
    own_half = lax.rem(chan_ref[0], 2)
    step_rows = high_ref.shape[0]
    own = pl.multiple_of(lead + own_half * half, math.gcd(lead, half))
    others = pl.multiple_of(lead + (1 - own_half) * half, math.gcd(lead, half))
    ext_ref[pl.ds(own, half), :] = mine_ref[...]
    ext_ref[pl.ds(others, half), :] = other_ref[...]
    end = lead + 2 * half
    if not first:
        ext_ref[:lead, :] = tail_in_ref[...]
    if last:
        ext_ref[end:, :] = after_ref[...]
    else:
        tail_out_ref[...] = ext_ref[end - MAXLAG : end, :]
    steps = (end if last else end - MAXLAG) // step_rows
    sum_ref[...] = jnp.zeros_like(sum_ref) if first else sum_in_ref[...]
    part = 128

    def step(i, _):
        start = i * step_rows
        for lag in range(lag_count):
            for row in range(0, step_rows, part):
                value = ext_ref[pl.ds(start + row + lags[lag], part), :]
                high = value.astype(jnp.bfloat16)
                high_ref[row : row + part, lag * NODES : (lag + 1) * NODES] = high
                low_ref[row : row + part, lag * NODES : (lag + 1) * NODES] = (
                    value - high.astype(jnp.float32)
                ).astype(jnp.bfloat16)

        def product(left, right):
            return lax.dot_general(left, right, CONTRACT_ROWS, preferred_element_type=jnp.float32)

        left = slice(0, 2 * NODES)
        total = product(high_ref[:, left], high_ref[...])
        total = total + product(high_ref[:, left], low_ref[...])
        total = total + product(low_ref[:, left], high_ref[...])
        sum_ref[...] += total
        return 0

    lax.fori_loop(0, steps, step, 0)
    if last:
        far = lag_count - 2
        for j in range(far):
            out_ref[j * NODES : (j + 1) * NODES, :] = sum_ref[:NODES, j * NODES : (j + 1) * NODES]
            place = (far + j) * NODES
            out_ref[place : place + NODES, :] = sum_ref[NODES:, (j + 1) * NODES : (j + 2) * NODES]
        which = jnp.where(4 * chan_ref[0] >= total_lags, 1, 0)
        row = pl.multiple_of(which * NODES, NODES)
        column = pl.multiple_of((far + which) * NODES, NODES)
        out_ref[2 * far * NODES :, :] = sum_ref[pl.ds(row, NODES), pl.ds(column, NODES)]
    else:
        out_ref[...] = sum_ref[...]


def gram_part(chan, lags, mine, other, carried, after, earlier):
    first, last = carried is None, after is not None
    count = lags.shape[0] // 2 + 2
    blocks = 2 * (count - 2) + 1
    operands = [chan, lags, mine, other]
    if not first:
        operands += list(carried)
    if last:
        operands.append(after)
    if last:
        out_shape = jax.ShapeDtypeStruct((blocks * NODES, NODES), jnp.float32)
    else:
        out_shape = (
            jax.ShapeDtypeStruct((2 * NODES, count * NODES), jnp.float32),
            jax.ShapeDtypeStruct((MAXLAG, NODES), jnp.float32),
        )
    rows = 2 * mine.shape[0] + (0 if first else MAXLAG) + (MAXLAG if last else 0)
    vmem = pl.BlockSpec(memory_space=pltpu.VMEM)
    smem = pl.BlockSpec(memory_space=pltpu.SMEM)
    step_rows = 512
    return pl.pallas_call(
        functools.partial(gram_kernel, first, last, len(earlier)),
        out_shape=out_shape,
        in_specs=[smem, smem] + [vmem] * (len(operands) - 2) + [pl.BlockSpec(memory_space=pl.ANY)] * len(earlier),
        out_specs=vmem if last else (vmem, vmem),
        scratch_shapes=[
            pltpu.VMEM((rows, NODES), jnp.float32),
            pltpu.VMEM((step_rows, count * NODES), jnp.bfloat16),
            pltpu.VMEM((step_rows, count * NODES), jnp.bfloat16),
            pltpu.VMEM((2 * NODES, count * NODES), jnp.float32),
        ],
        compiler_params=pltpu.CompilerParams(vmem_limit_bytes=40 << 20),
    )(*operands, *earlier)


def row_of(value, index):
    return jnp.broadcast_to(value[index : index + 1, :], value.shape)


def column_of(value, index):
    return jnp.broadcast_to(value[:, index : index + 1], value.shape)


def factor_block(block):
    count = len(block)
    sub = lax.broadcasted_iota(jnp.int32, (GROUP, BLOCK), 0)
    lane = lax.broadcasted_iota(jnp.int32, (GROUP, BLOCK), 1)
    state = list(block)
    result = [None] * count
    full = [None] * count
    columns = [column_of(state[0], m) for m in range(GROUP)]
    for g in range(count):
        first_lane, next_lane = GROUP * g, GROUP * (g + 1)
        here = (lane >= first_lane) & (lane < next_lane)
        span = g // SPAN
        more = g + 1 < count
        if more:
            next_columns = [column_of(state[g + 1], next_lane + m) for m in range(GROUP)]
            next_left = [column_of(state[g + 1], first_lane + m) for m in range(GROUP)]
            state[g + 1] = jnp.where(here, 0.0, state[g + 1])
        top = jnp.where(here, jnp.where(lane == sub + first_lane, 1.0, 0.0), state[g])
        diagonal = jnp.zeros_like(top)
        scale, factors, rows = [], {}, []
        for m in range(GROUP):
            pivot = row_of(columns[m], m)
            scale.append(lax.rsqrt(pivot))
            left = columns[m] * scale[m]
            for n in range(m + 1, GROUP):
                factors[m, n] = row_of(left, n)
                columns[n] = columns[n] - left * factors[m, n]
            if more:
                next_left[m] = next_left[m] * scale[m]
                for n in range(m + 1, GROUP):
                    next_left[n] = next_left[n] - next_left[m] * factors[m, n]
                for n in range(GROUP):
                    next_columns[n] = next_columns[n] - next_left[m] * row_of(next_left[m], n)
            rows.append(row_of(top, m) * scale[m])
            below = jnp.where(sub > m, left, 0.0)
            top = jnp.where(sub == m, rows[m], top - below * rows[m])
            entries = pivot * scale[m]
            for n in range(m + 1, GROUP):
                entries = jnp.where(lane == first_lane + n, factors[m, n], entries)
            diagonal = jnp.where(sub == m, entries, diagonal)
            if more:
                state[g + 1] = state[g + 1] - next_left[m] * rows[m]
        full[g] = top
        result[g] = jnp.where(lane >= next_lane, top, jnp.where(lane >= sub + first_lane, diagonal, 0.0))
        state[g] = jnp.where(lane < next_lane, top, 0.0)
        columns = next_columns
        for s in range(g + 2, min(count, (span + 2) * SPAN)):
            left = [column_of(state[s], first_lane + m) for m in range(GROUP)]
            value = jnp.where(here, 0.0, state[s])
            for m in range(GROUP):
                left[m] = left[m] * scale[m]
                for n in range(m + 1, GROUP):
                    left[n] = left[n] - left[m] * factors[m, n]
                value = value - left[m] * rows[m]
            state[s] = value
        rest = (span + 2) * SPAN
        if g % SPAN == SPAN - 1 and rest < count:
            begin = span * SPAN
            left = jnp.concatenate(full[begin : g + 1], axis=0)
            right = [
                jnp.where((lane >= GROUP * (i + 1)) & (lane < next_lane), 0.0, full[i]) for i in range(begin, g + 1)
            ]
            update = lax.dot_general(
                left[:, GROUP * rest :],
                jnp.concatenate(right, axis=0),
                CONTRACT_ROWS,
                precision=HIGHEST,
                preferred_element_type=jnp.float32,
            )
            inside = (lane >= GROUP * begin) & (lane < next_lane)
            for s in range(rest, count):
                place = GROUP * (s - rest)
                state[s] = jnp.where(inside, 0.0, state[s]) - update[place : place + GROUP]
    return result, state


def arrange(half_ref, mine_ref, other_ref, natural_ref, ordered_ref):
    chan_count = 4
    lag_count = 2 * chan_count
    far = lag_count // 2
    width = NODES // chan_count
    each = (2 * far + 1) * NODES

    def place(ref, low):
        for high in range(2):
            chan = 2 * high + low
            pairs = [(2 * chan + i, (2 * chan + i + d) % lag_count) for i in range(2) for d in range(far)]
            odd = 2 * chan // far
            pairs.append((2 * chan + odd, (2 * chan + odd + far) % lag_count))
            for index, (left, right) in enumerate(pairs):
                start = high * each + index * NODES
                block = ref[start : start + NODES, :]
                natural_ref[left * NODES : (left + 1) * NODES, right * NODES : (right + 1) * NODES] = block
                if left != right:
                    natural_ref[right * NODES : (right + 1) * NODES, left * NODES : (left + 1) * NODES] = block.T

    for low in range(2):

        @pl.when(half_ref[0] == low)
        def _():
            place(mine_ref, low)
            place(other_ref, 1 - low)

    lane_part = lax.broadcasted_iota(jnp.int32, (width, NODES), 1) // width

    def rows_of_lag(lag, _):
        for group in range(chan_count):
            source = pl.ds(pl.multiple_of(lag * NODES + group * width, width), width)
            target = pl.ds(pl.multiple_of(group * lag_count * width + lag * width, width), width)
            for half in range(2):
                parts = [natural_ref[source, (4 * half + i) * NODES : (4 * half + i + 1) * NODES] for i in range(4)]
                for other in range(group, chan_count):
                    block = None
                    for i in range(4):
                        shift = (i - other) % 4 * width
                        part = pltpu.roll(parts[i], shift, 1) if shift else parts[i]
                        block = part if block is None else jnp.where(lane_part == i, part, block)
                    column = (2 * other + half) * BLOCK
                    ordered_ref[target, column : column + BLOCK] = block
        return 0

    lax.fori_loop(0, lag_count, rows_of_lag, 0)


def cholesky_kernel(scale, half_ref, mine_ref, other_ref, out_ref, natural_ref, ordered_ref, panel_ref, inverse_ref):
    arrange(half_ref, mine_ref, other_ref, natural_ref, ordered_ref)
    size = out_ref.shape[0]
    count = size // BLOCK
    out_ref[...] = jnp.zeros_like(out_ref)

    def step(k, _):
        start = pl.multiple_of(k * BLOCK, BLOCK)
        for kk in range(count):

            @pl.when(k == kk)
            def _():
                mine = slice(kk * BLOCK, (kk + 1) * BLOCK)
                panel = ordered_ref[mine, kk * BLOCK :] * scale
                if kk:
                    panel = panel - lax.dot_general(
                        out_ref[: kk * BLOCK, mine],
                        out_ref[: kk * BLOCK, kk * BLOCK :],
                        CONTRACT_ROWS,
                        precision=HIGHEST,
                        preferred_element_type=jnp.float32,
                    )
                panel_ref[:, kk * BLOCK :] = panel

        block = [panel_ref[GROUP * s : GROUP * (s + 1), pl.ds(start, BLOCK)] for s in range(BLOCK // GROUP)]
        block, inverse = factor_block(block)
        for s in range(BLOCK // GROUP):
            out_ref[pl.ds(pl.multiple_of(start + GROUP * s, GROUP), GROUP), pl.ds(start, BLOCK)] = block[s]
            inverse_ref[GROUP * s : GROUP * (s + 1), :] = inverse[s]
        for kk in range(count - 1):

            @pl.when(k == kk)
            def _():
                out_ref[kk * BLOCK : (kk + 1) * BLOCK, (kk + 1) * BLOCK :] = jnp.dot(
                    inverse_ref[...],
                    panel_ref[:, (kk + 1) * BLOCK :],
                    precision=HIGHEST,
                    preferred_element_type=jnp.float32,
                )

        return 0

    lax.fori_loop(0, count, step, 0)


def cholesky(half, mine, other, size, scale):
    vmem = pl.BlockSpec(memory_space=pltpu.VMEM)
    return pl.pallas_call(
        functools.partial(cholesky_kernel, scale),
        out_shape=jax.ShapeDtypeStruct((size, size), jnp.float32),
        in_specs=[pl.BlockSpec(memory_space=pltpu.SMEM), vmem, vmem],
        out_specs=vmem,
        scratch_shapes=[
            pltpu.VMEM((size, size), jnp.float32),
            pltpu.VMEM((size, size), jnp.float32),
            pltpu.VMEM((BLOCK, size), jnp.float32),
            pltpu.VMEM((BLOCK, BLOCK), jnp.float32),
        ],
        compiler_params=pltpu.CompilerParams(vmem_limit_bytes=48 << 20),
    )(half, mine, other)


def on_device(signals, channel_node, lag_offsets):
    chan = lax.axis_index("chan").reshape(1)
    half = chan % 2
    send = project(signals, channel_node, 1 - half)
    received = swap(send, "chan", 1)
    keep = project(signals, channel_node, half)
    totals = add_parts(keep, received, CHUNKS)
    sent = [swap(total, "chan", 2) for total in totals]
    carried = after = None
    for index in range(CHUNKS):
        first, last = index == 0, index == CHUNKS - 1
        value = add(totals[index], sent[index], *(() if first else (carried[1], after)))
        other = swap(value, "chan", 1)
        if first:
            head = jnp.where(half[0] == 0, value[:MAXLAG], other[:MAXLAG])
            after = first_rows_of_next(head)
        earlier = (head,) if first else ()
        carried = gram_part(chan, lag_offsets, value, other, carried, after if last else None, earlier)
    blocks = sum_over_time_blocks(carried)
    blocks = double(blocks, "chan", 2)
    other = swap(blocks, "chan", 1)
    size = lag_offsets.shape[0] * NODES
    return cholesky(half, blocks, other, size, 1.0 / (signals.shape[0] * lax.axis_size("tm")))


def solution(mesh):
    return jax.shard_map(
        on_device, mesh=mesh, in_specs=(P("tm", "chan"), P("chan"), P()), out_specs=P(), check_vma=False
    )
```

```python
import functools
import math

import jax
import jax.numpy as jnp
from jax import lax
from jax.experimental import pallas as pl
from jax.experimental.pallas import tpu as pltpu
from jax.sharding import PartitionSpec as P

NODES = 128
CH = 2048
MAXLAG = 512
BLOCK = 128
GROUP = 8
SPAN = 4
CHUNKS = 2
HIGHEST = lax.Precision.HIGHEST
CONTRACT_ROWS = (((0,), (0,)), ((), ()))


def swap(value, axis, bit):
    count = lax.axis_size(axis)
    return lax.ppermute(value, axis, [(i, i ^ bit) for i in range(count)])


def bits_of(axis):
    count = lax.axis_size(axis)
    return [1 << i for i in range(count.bit_length() - 1)]


def halve(value, axis, bit):
    half = value.shape[0] // 2
    mine = (lax.axis_index(axis) // bit) % 2
    send = lax.dynamic_slice_in_dim(value, (1 - mine) * half, half, 0)
    keep = lax.dynamic_slice_in_dim(value, mine * half, half, 0)
    return keep + swap(send, axis, bit)


def double(value, axis, bit):
    mine = (lax.axis_index(axis) // bit) % 2
    other = swap(value, axis, bit)
    low = jnp.where(mine == 0, value, other)
    high = jnp.where(mine == 0, other, value)
    return jnp.concatenate([low, high], axis=0)


def sum_over_time_blocks(value):
    for bit in bits_of("tm"):
        value = halve(value, "tm", bit)
    for bit in bits_of("tm")[::-1]:
        value = double(value, "tm", bit)
    return value


def add_kernel(left_ref, right_ref, *refs):
    refs[-1][...] = left_ref[...] + right_ref[...]


def add(left, right, *earlier):
    vmem = pl.BlockSpec(memory_space=pltpu.VMEM)
    return pl.pallas_call(
        add_kernel,
        out_shape=jax.ShapeDtypeStruct(left.shape, left.dtype),
        in_specs=[vmem, vmem] + [pl.BlockSpec(memory_space=pl.ANY)] * len(earlier),
        out_specs=vmem,
        compiler_params=pltpu.CompilerParams(vmem_limit_bytes=8 << 20),
    )(left, right, *earlier)


def add_parts_kernel(left_ref, right_ref, *out_refs):
    start = 0
    for out_ref in out_refs:
        here = slice(start, start + out_ref.shape[0])
        out_ref[...] = left_ref[here, :] + right_ref[here, :]
        start += out_ref.shape[0]


def add_parts(left, right, parts):
    vmem = pl.BlockSpec(memory_space=pltpu.VMEM)
    part = jax.ShapeDtypeStruct((left.shape[0] // parts, left.shape[1]), left.dtype)
    return pl.pallas_call(
        add_parts_kernel,
        out_shape=(part,) * parts,
        in_specs=[vmem, vmem],
        out_specs=(vmem,) * parts,
        compiler_params=pltpu.CompilerParams(vmem_limit_bytes=8 << 20),
    )(left, right)


def first_rows_of_next(rows):
    count = lax.axis_size("tm")
    return lax.ppermute(rows, "tm", [(i, i - 1) for i in range(1, count)])


def project_kernel(half_ref, nodes_ref, signals_ref, out_ref, onehot_ref):
    @pl.when(pl.program_id(0) == 0)
    def _():
        node = lax.broadcasted_iota(jnp.int32, onehot_ref.shape, 0)
        scale = 1.0 / math.sqrt(CH // NODES)
        onehot_ref[...] = jnp.where(node == nodes_ref[...], scale, 0.0).astype(jnp.bfloat16)

    out_ref[...] = lax.dot_general(
        signals_ref[...], onehot_ref[...], (((1,), (1,)), ((), ())), preferred_element_type=jnp.float32
    )


def project(signals, channel_node, half):
    rows, channels = signals.shape
    part = rows // CHUNKS // 2
    step = min(512, part)
    steps = part // step
    grid_spec = pltpu.PrefetchScalarGridSpec(
        num_scalar_prefetch=1,
        grid=(CHUNKS * steps,),
        in_specs=[
            pl.BlockSpec((1, channels), lambda i, half: (0, 0)),
            pl.BlockSpec((step, channels), lambda i, half: ((i // steps * 2 + half[0]) * steps + i % steps, 0)),
        ],
        out_specs=pl.BlockSpec((step, NODES), lambda i, half: (i, 0)),
        scratch_shapes=[pltpu.VMEM((NODES, channels), jnp.bfloat16)],
    )
    return pl.pallas_call(
        project_kernel,
        out_shape=jax.ShapeDtypeStruct((rows // 2, NODES), jnp.float32),
        grid_spec=grid_spec,
        compiler_params=pltpu.CompilerParams(vmem_limit_bytes=8 << 20),
    )(half, channel_node.reshape(1, channels), signals)


def gram_kernel(first, last, earlier, chan_ref, all_lags_ref, *refs):
    refs = list(refs)
    mine_ref, other_ref = refs.pop(0), refs.pop(0)
    sum_in_ref, tail_in_ref = (None, None) if first else (refs.pop(0), refs.pop(0))
    after_ref = refs.pop(0) if last else None
    del refs[:earlier]
    out_ref = refs.pop(0)
    tail_out_ref = None if last else refs.pop(0)
    ext_ref, high_ref, low_ref, sum_ref = refs
    half = mine_ref.shape[0]
    lead = 0 if first else MAXLAG
    total_lags = all_lags_ref.shape[0]
    lag_count = sum_ref.shape[1] // NODES
    lags = [all_lags_ref[lax.rem(2 * chan_ref[0] + i, total_lags)] for i in range(lag_count)]
    own_half = lax.rem(chan_ref[0], 2)
    step_rows = high_ref.shape[0]
    own = pl.multiple_of(lead + own_half * half, math.gcd(lead, half))
    others = pl.multiple_of(lead + (1 - own_half) * half, math.gcd(lead, half))
    ext_ref[pl.ds(own, half), :] = mine_ref[...]
    ext_ref[pl.ds(others, half), :] = other_ref[...]
    end = lead + 2 * half
    if not first:
        ext_ref[:lead, :] = tail_in_ref[...]
    if last:
        ext_ref[end:, :] = after_ref[...]
    else:
        tail_out_ref[...] = ext_ref[end - MAXLAG : end, :]
    steps = (end if last else end - MAXLAG) // step_rows
    sum_ref[...] = jnp.zeros_like(sum_ref) if first else sum_in_ref[...]
    part = 128

    def step(i, _):
        start = i * step_rows
        for lag in range(lag_count):
            for row in range(0, step_rows, part):
                value = ext_ref[pl.ds(start + row + lags[lag], part), :]
                high = value.astype(jnp.bfloat16)
                high_ref[row : row + part, lag * NODES : (lag + 1) * NODES] = high
                low_ref[row : row + part, lag * NODES : (lag + 1) * NODES] = (
                    value - high.astype(jnp.float32)
                ).astype(jnp.bfloat16)

        def product(left, right):
            return lax.dot_general(left, right, CONTRACT_ROWS, preferred_element_type=jnp.float32)

        left = slice(0, 2 * NODES)
        total = product(high_ref[:, left], high_ref[...])
        total = total + product(high_ref[:, left], low_ref[...])
        total = total + product(low_ref[:, left], high_ref[...])
        sum_ref[...] += total
        return 0

    lax.fori_loop(0, steps, step, 0)
    if last:
        far = lag_count - 2
        for j in range(far):
            out_ref[j * NODES : (j + 1) * NODES, :] = sum_ref[:NODES, j * NODES : (j + 1) * NODES]
            place = (far + j) * NODES
            out_ref[place : place + NODES, :] = sum_ref[NODES:, (j + 1) * NODES : (j + 2) * NODES]
        which = jnp.where(4 * chan_ref[0] >= total_lags, 1, 0)
        row = pl.multiple_of(which * NODES, NODES)
        column = pl.multiple_of((far + which) * NODES, NODES)
        out_ref[2 * far * NODES :, :] = sum_ref[pl.ds(row, NODES), pl.ds(column, NODES)]
    else:
        out_ref[...] = sum_ref[...]


def gram_part(chan, lags, mine, other, carried, after, earlier):
    first, last = carried is None, after is not None
    count = lags.shape[0] // 2 + 2
    blocks = 2 * (count - 2) + 1
    operands = [chan, lags, mine, other]
    if not first:
        operands += list(carried)
    if last:
        operands.append(after)
    if last:
        out_shape = jax.ShapeDtypeStruct((blocks * NODES, NODES), jnp.float32)
    else:
        out_shape = (
            jax.ShapeDtypeStruct((2 * NODES, count * NODES), jnp.float32),
            jax.ShapeDtypeStruct((MAXLAG, NODES), jnp.float32),
        )
    rows = 2 * mine.shape[0] + (0 if first else MAXLAG) + (MAXLAG if last else 0)
    vmem = pl.BlockSpec(memory_space=pltpu.VMEM)
    smem = pl.BlockSpec(memory_space=pltpu.SMEM)
    step_rows = 512
    return pl.pallas_call(
        functools.partial(gram_kernel, first, last, len(earlier)),
        out_shape=out_shape,
        in_specs=[smem, smem] + [vmem] * (len(operands) - 2) + [pl.BlockSpec(memory_space=pl.ANY)] * len(earlier),
        out_specs=vmem if last else (vmem, vmem),
        scratch_shapes=[
            pltpu.VMEM((rows, NODES), jnp.float32),
            pltpu.VMEM((step_rows, count * NODES), jnp.bfloat16),
            pltpu.VMEM((step_rows, count * NODES), jnp.bfloat16),
            pltpu.VMEM((2 * NODES, count * NODES), jnp.float32),
        ],
        compiler_params=pltpu.CompilerParams(vmem_limit_bytes=12 << 20),
    )(*operands, *earlier)


def row_of(value, index):
    return jnp.broadcast_to(value[index : index + 1, :], value.shape)


def column_of(value, index):
    return jnp.broadcast_to(value[:, index : index + 1], value.shape)


def factor_block(block):
    count = len(block)
    sub = lax.broadcasted_iota(jnp.int32, (GROUP, BLOCK), 0)
    lane = lax.broadcasted_iota(jnp.int32, (GROUP, BLOCK), 1)
    state = list(block)
    result = [None] * count
    full = [None] * count
    columns = [column_of(state[0], m) for m in range(GROUP)]
    for g in range(count):
        first_lane, next_lane = GROUP * g, GROUP * (g + 1)
        here = (lane >= first_lane) & (lane < next_lane)
        span = g // SPAN
        more = g + 1 < count
        if more:
            next_columns = [column_of(state[g + 1], next_lane + m) for m in range(GROUP)]
            next_left = [column_of(state[g + 1], first_lane + m) for m in range(GROUP)]
            state[g + 1] = jnp.where(here, 0.0, state[g + 1])
        top = jnp.where(here, jnp.where(lane == sub + first_lane, 1.0, 0.0), state[g])
        diagonal = jnp.zeros_like(top)
        scale, factors, rows = [], {}, []
        for m in range(GROUP):
            pivot = row_of(columns[m], m)
            scale.append(lax.rsqrt(pivot))
            left = columns[m] * scale[m]
            for n in range(m + 1, GROUP):
                factors[m, n] = row_of(left, n)
                columns[n] = columns[n] - left * factors[m, n]
            if more:
                next_left[m] = next_left[m] * scale[m]
                for n in range(m + 1, GROUP):
                    next_left[n] = next_left[n] - next_left[m] * factors[m, n]
                for n in range(GROUP):
                    next_columns[n] = next_columns[n] - next_left[m] * row_of(next_left[m], n)
            rows.append(row_of(top, m) * scale[m])
            below = jnp.where(sub > m, left, 0.0)
            top = jnp.where(sub == m, rows[m], top - below * rows[m])
            entries = pivot * scale[m]
            for n in range(m + 1, GROUP):
                entries = jnp.where(lane == first_lane + n, factors[m, n], entries)
            diagonal = jnp.where(sub == m, entries, diagonal)
            if more:
                state[g + 1] = state[g + 1] - next_left[m] * rows[m]
        full[g] = top
        result[g] = jnp.where(lane >= next_lane, top, jnp.where(lane >= sub + first_lane, diagonal, 0.0))
        state[g] = jnp.where(lane < next_lane, top, 0.0)
        columns = next_columns
        for s in range(g + 2, min(count, (span + 2) * SPAN)):
            left = [column_of(state[s], first_lane + m) for m in range(GROUP)]
            value = jnp.where(here, 0.0, state[s])
            for m in range(GROUP):
                left[m] = left[m] * scale[m]
                for n in range(m + 1, GROUP):
                    left[n] = left[n] - left[m] * factors[m, n]
                value = value - left[m] * rows[m]
            state[s] = value
        rest = (span + 2) * SPAN
        if g % SPAN == SPAN - 1 and rest < count:
            begin = span * SPAN
            left = jnp.concatenate(full[begin : g + 1], axis=0)
            right = [
                jnp.where((lane >= GROUP * (i + 1)) & (lane < next_lane), 0.0, full[i]) for i in range(begin, g + 1)
            ]
            update = lax.dot_general(
                left[:, GROUP * rest :],
                jnp.concatenate(right, axis=0),
                CONTRACT_ROWS,
                precision=HIGHEST,
                preferred_element_type=jnp.float32,
            )
            inside = (lane >= GROUP * begin) & (lane < next_lane)
            for s in range(rest, count):
                place = GROUP * (s - rest)
                state[s] = jnp.where(inside, 0.0, state[s]) - update[place : place + GROUP]
    return result, state


def arrange(half_ref, mine_ref, other_ref, natural_ref, ordered_ref):
    chan_count = 4
    lag_count = 2 * chan_count
    far = lag_count // 2
    width = NODES // chan_count
    each = (2 * far + 1) * NODES

    def place(ref, low):
        for high in range(2):
            chan = 2 * high + low
            pairs = [(2 * chan + i, (2 * chan + i + d) % lag_count) for i in range(2) for d in range(far)]
            odd = 2 * chan // far
            pairs.append((2 * chan + odd, (2 * chan + odd + far) % lag_count))
            for index, (left, right) in enumerate(pairs):
                start = high * each + index * NODES
                block = ref[start : start + NODES, :]
                natural_ref[left * NODES : (left + 1) * NODES, right * NODES : (right + 1) * NODES] = block
                if left != right:
                    natural_ref[right * NODES : (right + 1) * NODES, left * NODES : (left + 1) * NODES] = block.T

    for low in range(2):

        @pl.when(half_ref[0] == low)
        def _():
            place(mine_ref, low)
            place(other_ref, 1 - low)

    lane_part = lax.broadcasted_iota(jnp.int32, (width, NODES), 1) // width

    def rows_of_lag(lag, _):
        for group in range(chan_count):
            source = pl.ds(pl.multiple_of(lag * NODES + group * width, width), width)
            target = pl.ds(pl.multiple_of(group * lag_count * width + lag * width, width), width)
            for half in range(2):
                parts = [natural_ref[source, (4 * half + i) * NODES : (4 * half + i + 1) * NODES] for i in range(4)]
                for other in range(group, chan_count):
                    block = None
                    for i in range(4):
                        shift = (i - other) % 4 * width
                        part = pltpu.roll(parts[i], shift, 1) if shift else parts[i]
                        block = part if block is None else jnp.where(lane_part == i, part, block)
                    column = (2 * other + half) * BLOCK
                    ordered_ref[target, column : column + BLOCK] = block
        return 0

    lax.fori_loop(0, lag_count, rows_of_lag, 0)


def cholesky_kernel(scale, half_ref, mine_ref, other_ref, out_ref, natural_ref, ordered_ref, panel_ref, inverse_ref):
    arrange(half_ref, mine_ref, other_ref, natural_ref, ordered_ref)
    size = out_ref.shape[0]
    count = size // BLOCK
    out_ref[...] = jnp.zeros_like(out_ref)

    def step(k, _):
        start = pl.multiple_of(k * BLOCK, BLOCK)
        for kk in range(count):

            @pl.when(k == kk)
            def _():
                mine = slice(kk * BLOCK, (kk + 1) * BLOCK)
                panel = ordered_ref[mine, kk * BLOCK :] * scale
                if kk:
                    panel = panel - lax.dot_general(
                        out_ref[: kk * BLOCK, mine],
                        out_ref[: kk * BLOCK, kk * BLOCK :],
                        CONTRACT_ROWS,
                        precision=HIGHEST,
                        preferred_element_type=jnp.float32,
                    )
                panel_ref[:, kk * BLOCK :] = panel

        block = [panel_ref[GROUP * s : GROUP * (s + 1), pl.ds(start, BLOCK)] for s in range(BLOCK // GROUP)]
        block, inverse = factor_block(block)
        for s in range(BLOCK // GROUP):
            out_ref[pl.ds(pl.multiple_of(start + GROUP * s, GROUP), GROUP), pl.ds(start, BLOCK)] = block[s]
            inverse_ref[GROUP * s : GROUP * (s + 1), :] = inverse[s]
        for kk in range(count - 1):

            @pl.when(k == kk)
            def _():
                out_ref[kk * BLOCK : (kk + 1) * BLOCK, (kk + 1) * BLOCK :] = jnp.dot(
                    inverse_ref[...],
                    panel_ref[:, (kk + 1) * BLOCK :],
                    precision=HIGHEST,
                    preferred_element_type=jnp.float32,
                )

        return 0

    lax.fori_loop(0, count, step, 0)


def cholesky(half, mine, other, size, scale):
    vmem = pl.BlockSpec(memory_space=pltpu.VMEM)
    return pl.pallas_call(
        functools.partial(cholesky_kernel, scale),
        out_shape=jax.ShapeDtypeStruct((size, size), jnp.float32),
        in_specs=[pl.BlockSpec(memory_space=pltpu.SMEM), vmem, vmem],
        out_specs=vmem,
        scratch_shapes=[
            pltpu.VMEM((size, size), jnp.float32),
            pltpu.VMEM((size, size), jnp.float32),
            pltpu.VMEM((BLOCK, size), jnp.float32),
            pltpu.VMEM((BLOCK, BLOCK), jnp.float32),
        ],
        compiler_params=pltpu.CompilerParams(vmem_limit_bytes=24 << 20),
    )(half, mine, other)


def on_device(signals, channel_node, lag_offsets):
    chan = lax.axis_index("chan").reshape(1)
    half = chan % 2
    send = project(signals, channel_node, 1 - half)
    received = swap(send, "chan", 1)
    keep = project(signals, channel_node, half)
    totals = add_parts(keep, received, CHUNKS)
    sent = [swap(total, "chan", 2) for total in totals]
    carried = after = None
    for index in range(CHUNKS):
        first, last = index == 0, index == CHUNKS - 1
        value = add(totals[index], sent[index], *(() if first else (carried[1], after)))
        other = swap(value, "chan", 1)
        if first:
            head = jnp.where(half[0] == 0, value[:MAXLAG], other[:MAXLAG])
            after = first_rows_of_next(head)
        earlier = (head,) if first else ()
        carried = gram_part(chan, lag_offsets, value, other, carried, after if last else None, earlier)
    blocks = sum_over_time_blocks(carried)
    blocks = double(blocks, "chan", 2)
    other = swap(blocks, "chan", 1)
    size = lag_offsets.shape[0] * NODES
    return cholesky(half, blocks, other, size, 1.0 / (signals.shape[0] * lax.axis_size("tm")))


def solution(mesh):
    return jax.shard_map(
        on_device, mesh=mesh, in_specs=(P("tm", "chan"), P("chan"), P()), out_specs=P(), check_vma=False
    )
```

```python
import functools
import math

import jax
import jax.numpy as jnp
from jax import lax
from jax.experimental import pallas as pl
from jax.experimental.pallas import tpu as pltpu
from jax.sharding import PartitionSpec as P

NODES = 128
CH = 2048
MAXLAG = 512
BLOCK = 128
GROUP = 8
SPAN = 4
CHUNK_QUARTERS = (1, 1)
HIGHEST = lax.Precision.HIGHEST
CONTRACT_ROWS = (((0,), (0,)), ((), ()))


def swap(value, axis, bit):
    count = lax.axis_size(axis)
    return lax.ppermute(value, axis, [(i, i ^ bit) for i in range(count)])


def bits_of(axis):
    count = lax.axis_size(axis)
    return [1 << i for i in range(count.bit_length() - 1)]


def halve(value, axis, bit):
    half = value.shape[0] // 2
    mine = (lax.axis_index(axis) // bit) % 2
    send = lax.dynamic_slice_in_dim(value, (1 - mine) * half, half, 0)
    keep = lax.dynamic_slice_in_dim(value, mine * half, half, 0)
    return keep + swap(send, axis, bit)


def double(value, axis, bit):
    mine = (lax.axis_index(axis) // bit) % 2
    other = swap(value, axis, bit)
    low = jnp.where(mine == 0, value, other)
    high = jnp.where(mine == 0, other, value)
    return jnp.concatenate([low, high], axis=0)


class Route:
    def __init__(self, scatter, gather):
        self.scatter, self.gather = scatter, gather

    def reduce(self, value):
        for bit in self.scatter:
            value = halve(value, "tm", bit)
        for axis, bit in self.gather:
            value = double(value, axis, bit)
        return value

    def pieces(self, rows, high):
        unit = rows >> len(self.scatter)
        found = []
        for index in range(1 << len(self.scatter)):
            value = {("chan", 2): high}
            for i, bit in enumerate(self.scatter):
                value["tm", bit] = index >> (len(self.scatter) - 1 - i) & 1
            place = sum(value[stage] << i for i, stage in enumerate(self.gather))
            found.append((index * unit, unit, place * unit))
        return found


def routes():
    bits = bits_of("tm")
    upper = ("chan", 2)
    first = Route(bits, [("tm", bit) for bit in bits[::-1]] + [upper])
    second = Route(bits[1:] + bits[:1], [upper] + [("tm", bit) for bit in bits[:0:-1] + bits[:1]])
    return first, second


def add_kernel(left_ref, right_ref, *refs):
    refs[-1][...] = left_ref[...] + right_ref[...]


def add(left, right, *earlier):
    vmem = pl.BlockSpec(memory_space=pltpu.VMEM)
    return pl.pallas_call(
        add_kernel,
        out_shape=jax.ShapeDtypeStruct(left.shape, left.dtype),
        in_specs=[vmem, vmem] + [pl.BlockSpec(memory_space=pl.ANY)] * len(earlier),
        out_specs=vmem,
        compiler_params=pltpu.CompilerParams(vmem_limit_bytes=8 << 20),
    )(left, right, *earlier)


def add_parts_kernel(left_ref, right_ref, *out_refs):
    start = 0
    for out_ref in out_refs:
        here = slice(start, start + out_ref.shape[0])
        out_ref[...] = left_ref[here, :] + right_ref[here, :]
        start += out_ref.shape[0]


def add_parts(left, right, sizes):
    vmem = pl.BlockSpec(memory_space=pltpu.VMEM)
    return pl.pallas_call(
        add_parts_kernel,
        out_shape=tuple(jax.ShapeDtypeStruct((size, left.shape[1]), left.dtype) for size in sizes),
        in_specs=[vmem, vmem],
        out_specs=(vmem,) * len(sizes),
        compiler_params=pltpu.CompilerParams(vmem_limit_bytes=8 << 20),
    )(left, right)


def first_rows_of_next(rows):
    count = lax.axis_size("tm")
    return lax.ppermute(rows, "tm", [(i, i - 1) for i in range(1, count)])


def project_kernel(half_ref, nodes_ref, signals_ref, out_ref, onehot_ref):
    @pl.when(pl.program_id(0) == 0)
    def _():
        node = lax.broadcasted_iota(jnp.int32, onehot_ref.shape, 0)
        scale = 1.0 / math.sqrt(CH // NODES)
        onehot_ref[...] = jnp.where(node == nodes_ref[...], scale, 0.0).astype(jnp.bfloat16)

    out_ref[...] = lax.dot_general(
        signals_ref[...], onehot_ref[...], (((1,), (1,)), ((), ())), preferred_element_type=jnp.float32
    )


def chunk_sizes(rows):
    return [rows * quarters // sum(CHUNK_QUARTERS) for quarters in CHUNK_QUARTERS]


def project(signals, channel_node, half):
    rows, channels = signals.shape
    parts = [size // 2 for size in chunk_sizes(rows)]
    step = math.gcd(512, *parts)
    steps = sum(parts) // step

    def block_of(i, half):
        done, block = 0, i
        for part in parts:
            count = part // step
            block = jnp.where(i >= done, done + i + half[0] * count, block)
            done += count
        return block, 0

    grid_spec = pltpu.PrefetchScalarGridSpec(
        num_scalar_prefetch=1,
        grid=(steps,),
        in_specs=[
            pl.BlockSpec((1, channels), lambda i, half: (0, 0)),
            pl.BlockSpec((step, channels), block_of),
        ],
        out_specs=pl.BlockSpec((step, NODES), lambda i, half: (i, 0)),
        scratch_shapes=[pltpu.VMEM((NODES, channels), jnp.bfloat16)],
    )
    return pl.pallas_call(
        project_kernel,
        out_shape=jax.ShapeDtypeStruct((rows // 2, NODES), jnp.float32),
        grid_spec=grid_spec,
        compiler_params=pltpu.CompilerParams(vmem_limit_bytes=8 << 20),
    )(half, channel_node.reshape(1, channels), signals)


def gram_kernel(first, last, earlier, chan_ref, all_lags_ref, *refs):
    refs = list(refs)
    mine_ref, other_ref = refs.pop(0), refs.pop(0)
    sum_in_ref, tail_in_ref = (None, None) if first else (refs.pop(0), refs.pop(0))
    after_ref = refs.pop(0) if last else None
    del refs[:earlier]
    out_ref = refs.pop(0)
    tail_out_ref = None if last else refs.pop(0)
    ext_ref, high_ref, low_ref, sum_ref = refs
    half = mine_ref.shape[0]
    lead = 0 if first else MAXLAG
    total_lags = all_lags_ref.shape[0]
    lag_count = sum_ref.shape[1] // NODES
    lags = [all_lags_ref[lax.rem(2 * chan_ref[0] + i, total_lags)] for i in range(lag_count)]
    own_half = lax.rem(chan_ref[0], 2)
    step_rows = high_ref.shape[0]
    own = pl.multiple_of(lead + own_half * half, math.gcd(lead, half))
    others = pl.multiple_of(lead + (1 - own_half) * half, math.gcd(lead, half))
    ext_ref[pl.ds(own, half), :] = mine_ref[...]
    ext_ref[pl.ds(others, half), :] = other_ref[...]
    end = lead + 2 * half
    if not first:
        ext_ref[:lead, :] = tail_in_ref[...]
    if last:
        ext_ref[end:, :] = after_ref[...]
    else:
        tail_out_ref[...] = ext_ref[end - MAXLAG : end, :]
    steps = (end if last else end - MAXLAG) // step_rows
    sum_ref[...] = jnp.zeros_like(sum_ref) if first else sum_in_ref[...]
    part = 128

    def step(i, _):
        start = i * step_rows
        for lag in range(lag_count):
            for row in range(0, step_rows, part):
                value = ext_ref[pl.ds(start + row + lags[lag], part), :]
                high = value.astype(jnp.bfloat16)
                high_ref[row : row + part, lag * NODES : (lag + 1) * NODES] = high
                low_ref[row : row + part, lag * NODES : (lag + 1) * NODES] = (
                    value - high.astype(jnp.float32)
                ).astype(jnp.bfloat16)

        def product(left, right):
            return lax.dot_general(left, right, CONTRACT_ROWS, preferred_element_type=jnp.float32)

        left = slice(0, 2 * NODES)
        total = product(high_ref[:, left], high_ref[...])
        total = total + product(high_ref[:, left], low_ref[...])
        total = total + product(low_ref[:, left], high_ref[...])
        sum_ref[...] += total
        return 0

    lax.fori_loop(0, steps, step, 0)
    if last:
        far = lag_count - 2
        for j in range(far):
            out_ref[j * NODES : (j + 1) * NODES, :] = sum_ref[:NODES, j * NODES : (j + 1) * NODES]
            place = (far + j) * NODES
            out_ref[place : place + NODES, :] = sum_ref[NODES:, (j + 1) * NODES : (j + 2) * NODES]
        which = jnp.where(4 * chan_ref[0] >= total_lags, 1, 0)
        row = pl.multiple_of(which * NODES, NODES)
        column = pl.multiple_of((far + which) * NODES, NODES)
        out_ref[2 * far * NODES :, :] = sum_ref[pl.ds(row, NODES), pl.ds(column, NODES)]
    else:
        out_ref[...] = sum_ref[...]


def gram_part(chan, lags, mine, other, carried, after, earlier):
    first, last = carried is None, after is not None
    count = lags.shape[0] // 2 + 2
    blocks = 2 * (count - 2) + 1
    operands = [chan, lags, mine, other]
    if not first:
        operands += list(carried)
    if last:
        operands.append(after)
    if last:
        out_shape = jax.ShapeDtypeStruct((blocks * NODES, NODES), jnp.float32)
    else:
        out_shape = (
            jax.ShapeDtypeStruct((2 * NODES, count * NODES), jnp.float32),
            jax.ShapeDtypeStruct((MAXLAG, NODES), jnp.float32),
        )
    rows = 2 * mine.shape[0] + (0 if first else MAXLAG) + (MAXLAG if last else 0)
    vmem = pl.BlockSpec(memory_space=pltpu.VMEM)
    smem = pl.BlockSpec(memory_space=pltpu.SMEM)
    step_rows = 512
    return pl.pallas_call(
        functools.partial(gram_kernel, first, last, len(earlier)),
        out_shape=out_shape,
        in_specs=[smem, smem] + [vmem] * (len(operands) - 2) + [pl.BlockSpec(memory_space=pl.ANY)] * len(earlier),
        out_specs=vmem if last else (vmem, vmem),
        scratch_shapes=[
            pltpu.VMEM((rows, NODES), jnp.float32),
            pltpu.VMEM((step_rows, count * NODES), jnp.bfloat16),
            pltpu.VMEM((step_rows, count * NODES), jnp.bfloat16),
            pltpu.VMEM((2 * NODES, count * NODES), jnp.float32),
        ],
        compiler_params=pltpu.CompilerParams(vmem_limit_bytes=12 << 20),
    )(*operands, *earlier)


def row_of(value, index):
    return jnp.broadcast_to(value[index : index + 1, :], value.shape)


def column_of(value, index):
    return jnp.broadcast_to(value[:, index : index + 1], value.shape)


def factor_block(block):
    count = len(block)
    sub = lax.broadcasted_iota(jnp.int32, (GROUP, BLOCK), 0)
    lane = lax.broadcasted_iota(jnp.int32, (GROUP, BLOCK), 1)
    state = list(block)
    result = [None] * count
    full = [None] * count
    columns = [column_of(state[0], m) for m in range(GROUP)]
    for g in range(count):
        first_lane, next_lane = GROUP * g, GROUP * (g + 1)
        here = (lane >= first_lane) & (lane < next_lane)
        span = g // SPAN
        more = g + 1 < count
        if more:
            next_columns = [column_of(state[g + 1], next_lane + m) for m in range(GROUP)]
            next_left = [column_of(state[g + 1], first_lane + m) for m in range(GROUP)]
            state[g + 1] = jnp.where(here, 0.0, state[g + 1])
        top = jnp.where(here, jnp.where(lane == sub + first_lane, 1.0, 0.0), state[g])
        diagonal = jnp.zeros_like(top)
        scale, factors, rows = [], {}, []
        for m in range(GROUP):
            pivot = row_of(columns[m], m)
            scale.append(lax.rsqrt(pivot))
            left = columns[m] * scale[m]
            for n in range(m + 1, GROUP):
                factors[m, n] = row_of(left, n)
                columns[n] = columns[n] - left * factors[m, n]
            if more:
                next_left[m] = next_left[m] * scale[m]
                for n in range(m + 1, GROUP):
                    next_left[n] = next_left[n] - next_left[m] * factors[m, n]
                for n in range(GROUP):
                    next_columns[n] = next_columns[n] - next_left[m] * row_of(next_left[m], n)
            rows.append(row_of(top, m) * scale[m])
            below = jnp.where(sub > m, left, 0.0)
            top = jnp.where(sub == m, rows[m], top - below * rows[m])
            entries = pivot * scale[m]
            for n in range(m + 1, GROUP):
                entries = jnp.where(lane == first_lane + n, factors[m, n], entries)
            diagonal = jnp.where(sub == m, entries, diagonal)
            if more:
                state[g + 1] = state[g + 1] - next_left[m] * rows[m]
        full[g] = top
        result[g] = jnp.where(lane >= next_lane, top, jnp.where(lane >= sub + first_lane, diagonal, 0.0))
        state[g] = jnp.where(lane < next_lane, top, 0.0)
        columns = next_columns
        for s in range(g + 2, min(count, (span + 2) * SPAN)):
            left = [column_of(state[s], first_lane + m) for m in range(GROUP)]
            value = jnp.where(here, 0.0, state[s])
            for m in range(GROUP):
                left[m] = left[m] * scale[m]
                for n in range(m + 1, GROUP):
                    left[n] = left[n] - left[m] * factors[m, n]
                value = value - left[m] * rows[m]
            state[s] = value
        rest = (span + 2) * SPAN
        if g % SPAN == SPAN - 1 and rest < count:
            begin = span * SPAN
            left = jnp.concatenate(full[begin : g + 1], axis=0)
            right = [
                jnp.where((lane >= GROUP * (i + 1)) & (lane < next_lane), 0.0, full[i]) for i in range(begin, g + 1)
            ]
            update = lax.dot_general(
                left[:, GROUP * rest :],
                jnp.concatenate(right, axis=0),
                CONTRACT_ROWS,
                precision=HIGHEST,
                preferred_element_type=jnp.float32,
            )
            inside = (lane >= GROUP * begin) & (lane < next_lane)
            for s in range(rest, count):
                place = GROUP * (s - rest)
                state[s] = jnp.where(inside, 0.0, state[s]) - update[place : place + GROUP]
    return result, state


def arrange(layout, half_ref, mine_refs, other_refs, natural_ref, ordered_ref):
    chan_count = 4
    lag_count = 2 * chan_count
    far = lag_count // 2
    width = NODES // chan_count

    def rows_of(refs, high, start, stop):
        found, base = [], 0
        for ref, pieces in zip(refs, layout):
            for first, count, place in pieces[high]:
                low, end = max(start, base + first), min(stop, base + first + count)
                if low < end:
                    offset = place - base - first
                    found.append(ref[low + offset : end + offset, :])
            base += ref.shape[0] // 2
        return found[0] if len(found) == 1 else jnp.concatenate(found, axis=0)

    def place(refs, low):
        for high in range(2):
            chan = 2 * high + low
            pairs = [(2 * chan + i, (2 * chan + i + d) % lag_count) for i in range(2) for d in range(far)]
            odd = 2 * chan // far
            pairs.append((2 * chan + odd, (2 * chan + odd + far) % lag_count))
            for index, (left, right) in enumerate(pairs):
                block = rows_of(refs, high, index * NODES, (index + 1) * NODES)
                natural_ref[left * NODES : (left + 1) * NODES, right * NODES : (right + 1) * NODES] = block
                if left != right:
                    natural_ref[right * NODES : (right + 1) * NODES, left * NODES : (left + 1) * NODES] = block.T

    for low in range(2):

        @pl.when(half_ref[0] == low)
        def _():
            place(mine_refs, low)
            place(other_refs, 1 - low)

    lane_part = lax.broadcasted_iota(jnp.int32, (width, NODES), 1) // width

    def rows_of_lag(lag, _):
        for group in range(chan_count):
            source = pl.ds(pl.multiple_of(lag * NODES + group * width, width), width)
            target = pl.ds(pl.multiple_of(group * lag_count * width + lag * width, width), width)
            for half in range(2):
                parts = [natural_ref[source, (4 * half + i) * NODES : (4 * half + i + 1) * NODES] for i in range(4)]
                for other in range(group, chan_count):
                    block = None
                    for i in range(4):
                        shift = (i - other) % 4 * width
                        part = pltpu.roll(parts[i], shift, 1) if shift else parts[i]
                        block = part if block is None else jnp.where(lane_part == i, part, block)
                    column = (2 * other + half) * BLOCK
                    ordered_ref[target, column : column + BLOCK] = block
        return 0

    lax.fori_loop(0, lag_count, rows_of_lag, 0)


def cholesky_kernel(scale, layout, half_ref, *refs):
    parts = len(layout)
    mine_refs, other_refs = refs[:parts], refs[parts : 2 * parts]
    out_ref, natural_ref, ordered_ref, panel_ref, inverse_ref = refs[2 * parts :]
    arrange(layout, half_ref, mine_refs, other_refs, natural_ref, ordered_ref)
    size = out_ref.shape[0]
    count = size // BLOCK
    out_ref[...] = jnp.zeros_like(out_ref)

    def step(k, _):
        start = pl.multiple_of(k * BLOCK, BLOCK)
        for kk in range(count):

            @pl.when(k == kk)
            def _():
                mine = slice(kk * BLOCK, (kk + 1) * BLOCK)
                panel = ordered_ref[mine, kk * BLOCK :] * scale
                if kk:
                    panel = panel - lax.dot_general(
                        out_ref[: kk * BLOCK, mine],
                        out_ref[: kk * BLOCK, kk * BLOCK :],
                        CONTRACT_ROWS,
                        precision=HIGHEST,
                        preferred_element_type=jnp.float32,
                    )
                panel_ref[:, kk * BLOCK :] = panel

        block = [panel_ref[GROUP * s : GROUP * (s + 1), pl.ds(start, BLOCK)] for s in range(BLOCK // GROUP)]
        block, inverse = factor_block(block)
        for s in range(BLOCK // GROUP):
            out_ref[pl.ds(pl.multiple_of(start + GROUP * s, GROUP), GROUP), pl.ds(start, BLOCK)] = block[s]
            inverse_ref[GROUP * s : GROUP * (s + 1), :] = inverse[s]
        for kk in range(count - 1):

            @pl.when(k == kk)
            def _():
                out_ref[kk * BLOCK : (kk + 1) * BLOCK, (kk + 1) * BLOCK :] = jnp.dot(
                    inverse_ref[...],
                    panel_ref[:, (kk + 1) * BLOCK :],
                    precision=HIGHEST,
                    preferred_element_type=jnp.float32,
                )

        return 0

    lax.fori_loop(0, count, step, 0)


def cholesky(half, mine, other, layout, size, scale):
    vmem = pl.BlockSpec(memory_space=pltpu.VMEM)
    return pl.pallas_call(
        functools.partial(cholesky_kernel, scale, layout),
        out_shape=jax.ShapeDtypeStruct((size, size), jnp.float32),
        in_specs=[pl.BlockSpec(memory_space=pltpu.SMEM)] + [vmem] * (2 * len(mine)),
        out_specs=vmem,
        scratch_shapes=[
            pltpu.VMEM((size, size), jnp.float32),
            pltpu.VMEM((size, size), jnp.float32),
            pltpu.VMEM((BLOCK, size), jnp.float32),
            pltpu.VMEM((BLOCK, BLOCK), jnp.float32),
        ],
        compiler_params=pltpu.CompilerParams(vmem_limit_bytes=24 << 20),
    )(half, *mine, *other)


def on_device(signals, channel_node, lag_offsets):
    chan = lax.axis_index("chan").reshape(1)
    half = chan % 2
    send = project(signals, channel_node, 1 - half)
    received = swap(send, "chan", 1)
    keep = project(signals, channel_node, half)
    sizes = chunk_sizes(signals.shape[0])
    totals = add_parts(keep, received, [size // 2 for size in sizes])
    sent = [swap(total, "chan", 2) for total in totals]
    carried = after = None
    for index in range(len(sizes)):
        first, last = index == 0, index == len(sizes) - 1
        value = add(totals[index], sent[index], *(() if first else (carried[1], after)))
        other = swap(value, "chan", 1)
        if first:
            head = jnp.where(half[0] == 0, value[:MAXLAG], other[:MAXLAG])
            after = first_rows_of_next(head)
        earlier = (head,) if first else ()
        carried = gram_part(chan, lag_offsets, value, other, carried, after if last else None, earlier)
    rows = carried.shape[0] // 2
    mine = [route.reduce(part) for route, part in zip(routes(), (carried[:rows], carried[rows:]))]
    other = [swap(value, "chan", 1) for value in mine]
    layout = [[route.pieces(rows, high) for high in range(2)] for route in routes()]
    size = lag_offsets.shape[0] * NODES
    return cholesky(half, mine, other, layout, size, 1.0 / (signals.shape[0] * lax.axis_size("tm")))


def solution(mesh):
    return jax.shard_map(
        on_device, mesh=mesh, in_specs=(P("tm", "chan"), P("chan"), P()), out_specs=P(), check_vma=False
    )
```

```python
import functools
import math

import jax
import jax.numpy as jnp
from jax import lax
from jax.experimental import pallas as pl
from jax.experimental.pallas import tpu as pltpu
from jax.sharding import PartitionSpec as P

NODES = 128
CH = 2048
MAXLAG = 512
BLOCK = 128
GROUP = 8
SPAN = 4
CHUNK_QUARTERS = (1, 1)
HIGHEST = lax.Precision.HIGHEST
CONTRACT_ROWS = (((0,), (0,)), ((), ()))


def swap(value, axis, bit):
    count = lax.axis_size(axis)
    return lax.ppermute(value, axis, [(i, i ^ bit) for i in range(count)])


def bits_of(axis):
    count = lax.axis_size(axis)
    return [1 << i for i in range(count.bit_length() - 1)]


def halve(value, axis, bit):
    half = value.shape[0] // 2
    mine = (lax.axis_index(axis) // bit) % 2
    send = lax.dynamic_slice_in_dim(value, (1 - mine) * half, half, 0)
    keep = lax.dynamic_slice_in_dim(value, mine * half, half, 0)
    return keep + swap(send, axis, bit)


def double(value, axis, bit):
    mine = (lax.axis_index(axis) // bit) % 2
    other = swap(value, axis, bit)
    low = jnp.where(mine == 0, value, other)
    high = jnp.where(mine == 0, other, value)
    return jnp.concatenate([low, high], axis=0)


class Route:
    def __init__(self, scatter, whole, gather):
        self.scatter, self.whole, self.gather = scatter, whole, gather

    def reduce(self, value):
        for bit in self.scatter:
            value = halve(value, "tm", bit)
        for bit in self.whole:
            value = value + swap(value, "tm", bit)
        for axis, bit in self.gather:
            value = double(value, axis, bit)
        return value

    def pieces(self, rows, high):
        unit = rows >> len(self.scatter)
        found = []
        for index in range(1 << len(self.scatter)):
            value = {("chan", 2): high}
            for i, bit in enumerate(self.scatter):
                value["tm", bit] = index >> (len(self.scatter) - 1 - i) & 1
            place = sum(value[stage] << i for i, stage in enumerate(self.gather))
            found.append((index * unit, unit, place * unit))
        return found


def routes():
    bits = bits_of("tm")
    upper = ("chan", 2)
    ahead, last = bits[:-1], bits[-1:]
    first = Route(ahead, last, [("tm", bit) for bit in ahead[::-1]] + [upper])
    turned = ahead[1:] + ahead[:1]
    second = Route(turned, last, [("tm", bit) for bit in turned[:0:-1]] + [upper] + [("tm", turned[0])])
    return first, second


def add_kernel(left_ref, right_ref, *refs):
    refs[-1][...] = left_ref[...] + right_ref[...]


def add(left, right, *earlier):
    vmem = pl.BlockSpec(memory_space=pltpu.VMEM)
    return pl.pallas_call(
        add_kernel,
        out_shape=jax.ShapeDtypeStruct(left.shape, left.dtype),
        in_specs=[vmem, vmem] + [pl.BlockSpec(memory_space=pl.ANY)] * len(earlier),
        out_specs=vmem,
        compiler_params=pltpu.CompilerParams(vmem_limit_bytes=8 << 20),
    )(left, right, *earlier)


def add_parts_kernel(left_ref, right_ref, *out_refs):
    start = 0
    for out_ref in out_refs:
        here = slice(start, start + out_ref.shape[0])
        out_ref[...] = left_ref[here, :] + right_ref[here, :]
        start += out_ref.shape[0]


def add_parts(left, right, sizes):
    vmem = pl.BlockSpec(memory_space=pltpu.VMEM)
    return pl.pallas_call(
        add_parts_kernel,
        out_shape=tuple(jax.ShapeDtypeStruct((size, left.shape[1]), left.dtype) for size in sizes),
        in_specs=[vmem, vmem],
        out_specs=(vmem,) * len(sizes),
        compiler_params=pltpu.CompilerParams(vmem_limit_bytes=8 << 20),
    )(left, right)


def first_rows_of_next(rows):
    count = lax.axis_size("tm")
    return lax.ppermute(rows, "tm", [(i, i - 1) for i in range(1, count)])


def project_kernel(half_ref, nodes_ref, signals_ref, out_ref, onehot_ref):
    @pl.when(pl.program_id(0) == 0)
    def _():
        node = lax.broadcasted_iota(jnp.int32, onehot_ref.shape, 0)
        scale = 1.0 / math.sqrt(CH // NODES)
        onehot_ref[...] = jnp.where(node == nodes_ref[...], scale, 0.0).astype(jnp.bfloat16)

    out_ref[...] = lax.dot_general(
        signals_ref[...], onehot_ref[...], (((1,), (1,)), ((), ())), preferred_element_type=jnp.float32
    )


def chunk_sizes(rows):
    return [rows * quarters // sum(CHUNK_QUARTERS) for quarters in CHUNK_QUARTERS]


def project(signals, channel_node, half):
    rows, channels = signals.shape
    parts = [size // 2 for size in chunk_sizes(rows)]
    step = math.gcd(512, *parts)
    steps = sum(parts) // step

    def block_of(i, half):
        done, block = 0, i
        for part in parts:
            count = part // step
            block = jnp.where(i >= done, done + i + half[0] * count, block)
            done += count
        return block, 0

    grid_spec = pltpu.PrefetchScalarGridSpec(
        num_scalar_prefetch=1,
        grid=(steps,),
        in_specs=[
            pl.BlockSpec((1, channels), lambda i, half: (0, 0)),
            pl.BlockSpec((step, channels), block_of),
        ],
        out_specs=pl.BlockSpec((step, NODES), lambda i, half: (i, 0)),
        scratch_shapes=[pltpu.VMEM((NODES, channels), jnp.bfloat16)],
    )
    return pl.pallas_call(
        project_kernel,
        out_shape=jax.ShapeDtypeStruct((rows // 2, NODES), jnp.float32),
        grid_spec=grid_spec,
        compiler_params=pltpu.CompilerParams(vmem_limit_bytes=8 << 20),
    )(half, channel_node.reshape(1, channels), signals)


def gram_kernel(first, last, earlier, chan_ref, all_lags_ref, *refs):
    refs = list(refs)
    mine_ref, other_ref = refs.pop(0), refs.pop(0)
    sum_in_ref, tail_in_ref = (None, None) if first else (refs.pop(0), refs.pop(0))
    after_ref = refs.pop(0) if last else None
    del refs[:earlier]
    out_ref = refs.pop(0)
    tail_out_ref = None if last else refs.pop(0)
    ext_ref, high_ref, low_ref, sum_ref = refs
    half = mine_ref.shape[0]
    lead = 0 if first else MAXLAG
    total_lags = all_lags_ref.shape[0]
    lag_count = sum_ref.shape[1] // NODES
    lags = [all_lags_ref[lax.rem(2 * chan_ref[0] + i, total_lags)] for i in range(lag_count)]
    own_half = lax.rem(chan_ref[0], 2)
    step_rows = high_ref.shape[0]
    own = pl.multiple_of(lead + own_half * half, math.gcd(lead, half))
    others = pl.multiple_of(lead + (1 - own_half) * half, math.gcd(lead, half))
    ext_ref[pl.ds(own, half), :] = mine_ref[...]
    ext_ref[pl.ds(others, half), :] = other_ref[...]
    end = lead + 2 * half
    if not first:
        ext_ref[:lead, :] = tail_in_ref[...]
    if last:
        ext_ref[end:, :] = after_ref[...]
    else:
        tail_out_ref[...] = ext_ref[end - MAXLAG : end, :]
    steps = (end if last else end - MAXLAG) // step_rows
    sum_ref[...] = jnp.zeros_like(sum_ref) if first else sum_in_ref[...]
    part = 128

    def step(i, _):
        start = i * step_rows
        for lag in range(lag_count):
            for row in range(0, step_rows, part):
                value = ext_ref[pl.ds(start + row + lags[lag], part), :]
                high = value.astype(jnp.bfloat16)
                high_ref[row : row + part, lag * NODES : (lag + 1) * NODES] = high
                low_ref[row : row + part, lag * NODES : (lag + 1) * NODES] = (
                    value - high.astype(jnp.float32)
                ).astype(jnp.bfloat16)

        def product(left, right):
            return lax.dot_general(left, right, CONTRACT_ROWS, preferred_element_type=jnp.float32)

        left = slice(0, 2 * NODES)
        total = product(high_ref[:, left], high_ref[...])
        total = total + product(high_ref[:, left], low_ref[...])
        total = total + product(low_ref[:, left], high_ref[...])
        sum_ref[...] += total
        return 0

    lax.fori_loop(0, steps, step, 0)
    if last:
        far = lag_count - 2
        for j in range(far):
            out_ref[j * NODES : (j + 1) * NODES, :] = sum_ref[:NODES, j * NODES : (j + 1) * NODES]
            place = (far + j) * NODES
            out_ref[place : place + NODES, :] = sum_ref[NODES:, (j + 1) * NODES : (j + 2) * NODES]
        which = jnp.where(4 * chan_ref[0] >= total_lags, 1, 0)
        row = pl.multiple_of(which * NODES, NODES)
        column = pl.multiple_of((far + which) * NODES, NODES)
        out_ref[2 * far * NODES :, :] = sum_ref[pl.ds(row, NODES), pl.ds(column, NODES)]
    else:
        out_ref[...] = sum_ref[...]


def gram_part(chan, lags, mine, other, carried, after, earlier):
    first, last = carried is None, after is not None
    count = lags.shape[0] // 2 + 2
    blocks = 2 * (count - 2) + 1
    operands = [chan, lags, mine, other]
    if not first:
        operands += list(carried)
    if last:
        operands.append(after)
    if last:
        out_shape = jax.ShapeDtypeStruct((blocks * NODES, NODES), jnp.float32)
    else:
        out_shape = (
            jax.ShapeDtypeStruct((2 * NODES, count * NODES), jnp.float32),
            jax.ShapeDtypeStruct((MAXLAG, NODES), jnp.float32),
        )
    rows = 2 * mine.shape[0] + (0 if first else MAXLAG) + (MAXLAG if last else 0)
    vmem = pl.BlockSpec(memory_space=pltpu.VMEM)
    smem = pl.BlockSpec(memory_space=pltpu.SMEM)
    step_rows = 512
    return pl.pallas_call(
        functools.partial(gram_kernel, first, last, len(earlier)),
        out_shape=out_shape,
        in_specs=[smem, smem] + [vmem] * (len(operands) - 2) + [pl.BlockSpec(memory_space=pl.ANY)] * len(earlier),
        out_specs=vmem if last else (vmem, vmem),
        scratch_shapes=[
            pltpu.VMEM((rows, NODES), jnp.float32),
            pltpu.VMEM((step_rows, count * NODES), jnp.bfloat16),
            pltpu.VMEM((step_rows, count * NODES), jnp.bfloat16),
            pltpu.VMEM((2 * NODES, count * NODES), jnp.float32),
        ],
        compiler_params=pltpu.CompilerParams(vmem_limit_bytes=12 << 20),
    )(*operands, *earlier)


def row_of(value, index):
    return jnp.broadcast_to(value[index : index + 1, :], value.shape)


def column_of(value, index):
    return jnp.broadcast_to(value[:, index : index + 1], value.shape)


def factor_block(block):
    count = len(block)
    sub = lax.broadcasted_iota(jnp.int32, (GROUP, BLOCK), 0)
    lane = lax.broadcasted_iota(jnp.int32, (GROUP, BLOCK), 1)
    state = list(block)
    result = [None] * count
    full = [None] * count
    columns = [column_of(state[0], m) for m in range(GROUP)]
    for g in range(count):
        first_lane, next_lane = GROUP * g, GROUP * (g + 1)
        here = (lane >= first_lane) & (lane < next_lane)
        span = g // SPAN
        more = g + 1 < count
        if more:
            next_columns = [column_of(state[g + 1], next_lane + m) for m in range(GROUP)]
            next_left = [column_of(state[g + 1], first_lane + m) for m in range(GROUP)]
            state[g + 1] = jnp.where(here, 0.0, state[g + 1])
        top = jnp.where(here, jnp.where(lane == sub + first_lane, 1.0, 0.0), state[g])
        diagonal = jnp.zeros_like(top)
        scale, factors, rows = [], {}, []
        for m in range(GROUP):
            pivot = row_of(columns[m], m)
            scale.append(lax.rsqrt(pivot))
            left = columns[m] * scale[m]
            for n in range(m + 1, GROUP):
                factors[m, n] = row_of(left, n)
                columns[n] = columns[n] - left * factors[m, n]
            if more:
                next_left[m] = next_left[m] * scale[m]
                for n in range(m + 1, GROUP):
                    next_left[n] = next_left[n] - next_left[m] * factors[m, n]
                for n in range(GROUP):
                    next_columns[n] = next_columns[n] - next_left[m] * row_of(next_left[m], n)
            rows.append(row_of(top, m) * scale[m])
            below = jnp.where(sub > m, left, 0.0)
            top = jnp.where(sub == m, rows[m], top - below * rows[m])
            entries = pivot * scale[m]
            for n in range(m + 1, GROUP):
                entries = jnp.where(lane == first_lane + n, factors[m, n], entries)
            diagonal = jnp.where(sub == m, entries, diagonal)
            if more:
                state[g + 1] = state[g + 1] - next_left[m] * rows[m]
        full[g] = top
        result[g] = jnp.where(lane >= next_lane, top, jnp.where(lane >= sub + first_lane, diagonal, 0.0))
        state[g] = jnp.where(lane < next_lane, top, 0.0)
        columns = next_columns
        for s in range(g + 2, min(count, (span + 2) * SPAN)):
            left = [column_of(state[s], first_lane + m) for m in range(GROUP)]
            value = jnp.where(here, 0.0, state[s])
            for m in range(GROUP):
                left[m] = left[m] * scale[m]
                for n in range(m + 1, GROUP):
                    left[n] = left[n] - left[m] * factors[m, n]
                value = value - left[m] * rows[m]
            state[s] = value
        rest = (span + 2) * SPAN
        if g % SPAN == SPAN - 1 and rest < count:
            begin = span * SPAN
            left = jnp.concatenate(full[begin : g + 1], axis=0)
            right = [
                jnp.where((lane >= GROUP * (i + 1)) & (lane < next_lane), 0.0, full[i]) for i in range(begin, g + 1)
            ]
            update = lax.dot_general(
                left[:, GROUP * rest :],
                jnp.concatenate(right, axis=0),
                CONTRACT_ROWS,
                precision=HIGHEST,
                preferred_element_type=jnp.float32,
            )
            inside = (lane >= GROUP * begin) & (lane < next_lane)
            for s in range(rest, count):
                place = GROUP * (s - rest)
                state[s] = jnp.where(inside, 0.0, state[s]) - update[place : place + GROUP]
    return result, state


def arrange(layout, half_ref, mine_refs, other_refs, natural_ref, ordered_ref):
    chan_count = 4
    lag_count = 2 * chan_count
    far = lag_count // 2
    width = NODES // chan_count

    def rows_of(refs, high, start, stop):
        found, base = [], 0
        for ref, pieces in zip(refs, layout):
            for first, count, place in pieces[high]:
                low, end = max(start, base + first), min(stop, base + first + count)
                if low < end:
                    offset = place - base - first
                    found.append(ref[low + offset : end + offset, :])
            base += ref.shape[0] // 2
        return found[0] if len(found) == 1 else jnp.concatenate(found, axis=0)

    def place(refs, low):
        for high in range(2):
            chan = 2 * high + low
            pairs = [(2 * chan + i, (2 * chan + i + d) % lag_count) for i in range(2) for d in range(far)]
            odd = 2 * chan // far
            pairs.append((2 * chan + odd, (2 * chan + odd + far) % lag_count))
            for index, (left, right) in enumerate(pairs):
                block = rows_of(refs, high, index * NODES, (index + 1) * NODES)
                natural_ref[left * NODES : (left + 1) * NODES, right * NODES : (right + 1) * NODES] = block
                if left != right:
                    natural_ref[right * NODES : (right + 1) * NODES, left * NODES : (left + 1) * NODES] = block.T

    for low in range(2):

        @pl.when(half_ref[0] == low)
        def _():
            place(mine_refs, low)
            place(other_refs, 1 - low)

    lane_part = lax.broadcasted_iota(jnp.int32, (width, NODES), 1) // width

    def rows_of_lag(lag, _):
        for group in range(chan_count):
            source = pl.ds(pl.multiple_of(lag * NODES + group * width, width), width)
            target = pl.ds(pl.multiple_of(group * lag_count * width + lag * width, width), width)
            for half in range(2):
                parts = [natural_ref[source, (4 * half + i) * NODES : (4 * half + i + 1) * NODES] for i in range(4)]
                for other in range(group, chan_count):
                    block = None
                    for i in range(4):
                        shift = (i - other) % 4 * width
                        part = pltpu.roll(parts[i], shift, 1) if shift else parts[i]
                        block = part if block is None else jnp.where(lane_part == i, part, block)
                    column = (2 * other + half) * BLOCK
                    ordered_ref[target, column : column + BLOCK] = block
        return 0

    lax.fori_loop(0, lag_count, rows_of_lag, 0)


def cholesky_kernel(scale, layout, half_ref, *refs):
    parts = len(layout)
    mine_refs, other_refs = refs[:parts], refs[parts : 2 * parts]
    out_ref, natural_ref, ordered_ref, panel_ref, inverse_ref = refs[2 * parts :]
    arrange(layout, half_ref, mine_refs, other_refs, natural_ref, ordered_ref)
    size = out_ref.shape[0]
    count = size // BLOCK
    out_ref[...] = jnp.zeros_like(out_ref)

    def step(k, _):
        start = pl.multiple_of(k * BLOCK, BLOCK)
        for kk in range(count):

            @pl.when(k == kk)
            def _():
                mine = slice(kk * BLOCK, (kk + 1) * BLOCK)
                panel = ordered_ref[mine, kk * BLOCK :] * scale
                if kk:
                    panel = panel - lax.dot_general(
                        out_ref[: kk * BLOCK, mine],
                        out_ref[: kk * BLOCK, kk * BLOCK :],
                        CONTRACT_ROWS,
                        precision=HIGHEST,
                        preferred_element_type=jnp.float32,
                    )
                panel_ref[:, kk * BLOCK :] = panel

        block = [panel_ref[GROUP * s : GROUP * (s + 1), pl.ds(start, BLOCK)] for s in range(BLOCK // GROUP)]
        block, inverse = factor_block(block)
        for s in range(BLOCK // GROUP):
            out_ref[pl.ds(pl.multiple_of(start + GROUP * s, GROUP), GROUP), pl.ds(start, BLOCK)] = block[s]
            inverse_ref[GROUP * s : GROUP * (s + 1), :] = inverse[s]
        for kk in range(count - 1):

            @pl.when(k == kk)
            def _():
                out_ref[kk * BLOCK : (kk + 1) * BLOCK, (kk + 1) * BLOCK :] = jnp.dot(
                    inverse_ref[...],
                    panel_ref[:, (kk + 1) * BLOCK :],
                    precision=HIGHEST,
                    preferred_element_type=jnp.float32,
                )

        return 0

    lax.fori_loop(0, count, step, 0)


def cholesky(half, mine, other, layout, size, scale):
    vmem = pl.BlockSpec(memory_space=pltpu.VMEM)
    return pl.pallas_call(
        functools.partial(cholesky_kernel, scale, layout),
        out_shape=jax.ShapeDtypeStruct((size, size), jnp.float32),
        in_specs=[pl.BlockSpec(memory_space=pltpu.SMEM)] + [vmem] * (2 * len(mine)),
        out_specs=vmem,
        scratch_shapes=[
            pltpu.VMEM((size, size), jnp.float32),
            pltpu.VMEM((size, size), jnp.float32),
            pltpu.VMEM((BLOCK, size), jnp.float32),
            pltpu.VMEM((BLOCK, BLOCK), jnp.float32),
        ],
        compiler_params=pltpu.CompilerParams(vmem_limit_bytes=24 << 20),
    )(half, *mine, *other)


def on_device(signals, channel_node, lag_offsets):
    chan = lax.axis_index("chan").reshape(1)
    half = chan % 2
    send = project(signals, channel_node, 1 - half)
    received = swap(send, "chan", 1)
    keep = project(signals, channel_node, half)
    sizes = chunk_sizes(signals.shape[0])
    totals = add_parts(keep, received, [size // 2 for size in sizes])
    sent = [swap(total, "chan", 2) for total in totals]
    carried = after = None
    for index in range(len(sizes)):
        first, last = index == 0, index == len(sizes) - 1
        value = add(totals[index], sent[index], *(() if first else (carried[1], after)))
        other = swap(value, "chan", 1)
        if first:
            head = jnp.where(half[0] == 0, value[:MAXLAG], other[:MAXLAG])
            after = first_rows_of_next(head)
        earlier = (head,) if first else ()
        carried = gram_part(chan, lag_offsets, value, other, carried, after if last else None, earlier)
    rows = carried.shape[0] // 2
    mine = [route.reduce(part) for route, part in zip(routes(), (carried[:rows], carried[rows:]))]
    other = [swap(value, "chan", 1) for value in mine]
    layout = [[route.pieces(rows, high) for high in range(2)] for route in routes()]
    size = lag_offsets.shape[0] * NODES
    return cholesky(half, mine, other, layout, size, 1.0 / (signals.shape[0] * lax.axis_size("tm")))


def solution(mesh):
    return jax.shard_map(
        on_device, mesh=mesh, in_specs=(P("tm", "chan"), P("chan"), P()), out_specs=P(), check_vma=False
    )
```

```python
import functools
import math

import jax
import jax.numpy as jnp
from jax import lax
from jax.experimental import pallas as pl
from jax.experimental.pallas import tpu as pltpu
from jax.sharding import PartitionSpec as P

NODES = 128
CH = 2048
MAXLAG = 512
BLOCK = 128
GROUP = 8
SPAN = 4
CHUNK_QUARTERS = (1, 1)
HIGHEST = lax.Precision.HIGHEST
CONTRACT_ROWS = (((0,), (0,)), ((), ()))


def swap(value, axis, bit):
    count = lax.axis_size(axis)
    return lax.ppermute(value, axis, [(i, i ^ bit) for i in range(count)])


def bits_of(axis):
    count = lax.axis_size(axis)
    return [1 << i for i in range(count.bit_length() - 1)]


def halve(value, axis, bit):
    half = value.shape[0] // 2
    mine = (lax.axis_index(axis) // bit) % 2
    send = lax.dynamic_slice_in_dim(value, (1 - mine) * half, half, 0)
    keep = lax.dynamic_slice_in_dim(value, mine * half, half, 0)
    return keep + swap(send, axis, bit)


def double(value, axis, bit):
    mine = (lax.axis_index(axis) // bit) % 2
    other = swap(value, axis, bit)
    low = jnp.where(mine == 0, value, other)
    high = jnp.where(mine == 0, other, value)
    return jnp.concatenate([low, high], axis=0)


class Route:
    def __init__(self, scatter, whole, gather):
        self.scatter, self.whole, self.gather = scatter, whole, gather

    def reduce(self, value):
        for bit in self.scatter:
            value = halve(value, "tm", bit)
        for bit in self.whole:
            value = value + swap(value, "tm", bit)
        for axis, bit in self.gather:
            value = double(value, axis, bit)
        return value

    def pieces(self, rows, high):
        unit = rows >> len(self.scatter)
        found = []
        for index in range(1 << len(self.scatter)):
            value = {("chan", 2): high}
            for i, bit in enumerate(self.scatter):
                value["tm", bit] = index >> (len(self.scatter) - 1 - i) & 1
            place = sum(value[stage] << i for i, stage in enumerate(self.gather))
            found.append((index * unit, unit, place * unit))
        return found


def routes():
    bits = bits_of("tm")
    upper = ("chan", 2)
    ahead, last = bits[:-1], bits[-1:]
    first = Route(ahead, last, [("tm", bit) for bit in ahead[::-1]] + [upper])
    turned = ahead[1:] + ahead[:1]
    second = Route(turned, last, [("tm", bit) for bit in turned[:0:-1]] + [upper] + [("tm", turned[0])])
    return first, second


def add_kernel(left_ref, right_ref, *refs):
    refs[-1][...] = left_ref[...] + right_ref[...]


def add(left, right, *earlier):
    vmem = pl.BlockSpec(memory_space=pltpu.VMEM)
    return pl.pallas_call(
        add_kernel,
        out_shape=jax.ShapeDtypeStruct(left.shape, left.dtype),
        in_specs=[vmem, vmem] + [pl.BlockSpec(memory_space=pl.ANY)] * len(earlier),
        out_specs=vmem,
        compiler_params=pltpu.CompilerParams(vmem_limit_bytes=8 << 20),
    )(left, right, *earlier)


def add_parts_kernel(left_ref, right_ref, *out_refs):
    start = 0
    for out_ref in out_refs:
        here = slice(start, start + out_ref.shape[0])
        out_ref[...] = left_ref[here, :] + right_ref[here, :]
        start += out_ref.shape[0]


def add_parts(left, right, sizes):
    vmem = pl.BlockSpec(memory_space=pltpu.VMEM)
    return pl.pallas_call(
        add_parts_kernel,
        out_shape=tuple(jax.ShapeDtypeStruct((size, left.shape[1]), left.dtype) for size in sizes),
        in_specs=[vmem, vmem],
        out_specs=(vmem,) * len(sizes),
        compiler_params=pltpu.CompilerParams(vmem_limit_bytes=8 << 20),
    )(left, right)


def first_rows_of_next(rows):
    count = lax.axis_size("tm")
    return lax.ppermute(rows, "tm", [(i, i - 1) for i in range(1, count)])


def project_kernel(half_ref, nodes_ref, signals_ref, out_ref, onehot_ref):
    @pl.when(pl.program_id(0) == 0)
    def _():
        node = lax.broadcasted_iota(jnp.int32, onehot_ref.shape, 0)
        scale = 1.0 / math.sqrt(CH // NODES)
        onehot_ref[...] = jnp.where(node == nodes_ref[...], scale, 0.0).astype(jnp.bfloat16)

    out_ref[...] = lax.dot_general(
        signals_ref[...], onehot_ref[...], (((1,), (1,)), ((), ())), preferred_element_type=jnp.float32
    )


def chunk_sizes(rows):
    return [rows * quarters // sum(CHUNK_QUARTERS) for quarters in CHUNK_QUARTERS]


def project(signals, channel_node, half):
    rows, channels = signals.shape
    parts = [size // 2 for size in chunk_sizes(rows)]
    step = math.gcd(512, *parts)
    steps = sum(parts) // step

    def block_of(i, half):
        done, block = 0, i
        for part in parts:
            count = part // step
            block = jnp.where(i >= done, done + i + half[0] * count, block)
            done += count
        return block, 0

    grid_spec = pltpu.PrefetchScalarGridSpec(
        num_scalar_prefetch=1,
        grid=(steps,),
        in_specs=[
            pl.BlockSpec((1, channels), lambda i, half: (0, 0)),
            pl.BlockSpec((step, channels), block_of),
        ],
        out_specs=pl.BlockSpec((step, NODES), lambda i, half: (i, 0)),
        scratch_shapes=[pltpu.VMEM((NODES, channels), jnp.bfloat16)],
    )
    return pl.pallas_call(
        project_kernel,
        out_shape=jax.ShapeDtypeStruct((rows // 2, NODES), jnp.float32),
        grid_spec=grid_spec,
        compiler_params=pltpu.CompilerParams(vmem_limit_bytes=8 << 20),
    )(half, channel_node.reshape(1, channels), signals)


def gram_kernel(first, last, earlier, chan_ref, all_lags_ref, *refs):
    refs = list(refs)
    mine_ref, other_ref = refs.pop(0), refs.pop(0)
    sum_in_ref, tail_in_ref = (None, None) if first else (refs.pop(0), refs.pop(0))
    after_ref = refs.pop(0) if last else None
    del refs[:earlier]
    out_ref = refs.pop(0)
    tail_out_ref = None if last else refs.pop(0)
    ext_ref, high_ref, low_ref, sum_ref = refs
    half = mine_ref.shape[0]
    lead = 0 if first else MAXLAG
    total_lags = all_lags_ref.shape[0]
    lag_count = sum_ref.shape[1] // NODES
    lags = [all_lags_ref[lax.rem(2 * chan_ref[0] + i, total_lags)] for i in range(lag_count)]
    own_half = lax.rem(chan_ref[0], 2)
    step_rows = high_ref.shape[0]
    own = pl.multiple_of(lead + own_half * half, math.gcd(lead, half))
    others = pl.multiple_of(lead + (1 - own_half) * half, math.gcd(lead, half))
    ext_ref[pl.ds(own, half), :] = mine_ref[...]
    ext_ref[pl.ds(others, half), :] = other_ref[...]
    end = lead + 2 * half
    if not first:
        ext_ref[:lead, :] = tail_in_ref[...]
    if last:
        ext_ref[end:, :] = after_ref[...]
    else:
        tail_out_ref[...] = ext_ref[end - MAXLAG : end, :]
    steps = (end if last else end - MAXLAG) // step_rows
    sum_ref[...] = jnp.zeros_like(sum_ref) if first else sum_in_ref[...]
    part = 128

    def step(i, _):
        start = i * step_rows
        for lag in range(lag_count):
            for row in range(0, step_rows, part):
                value = ext_ref[pl.ds(start + row + lags[lag], part), :]
                high = value.astype(jnp.bfloat16)
                high_ref[row : row + part, lag * NODES : (lag + 1) * NODES] = high
                low_ref[row : row + part, lag * NODES : (lag + 1) * NODES] = (
                    value - high.astype(jnp.float32)
                ).astype(jnp.bfloat16)

        def product(left, right):
            return lax.dot_general(left, right, CONTRACT_ROWS, preferred_element_type=jnp.float32)

        left = slice(0, 2 * NODES)
        total = product(high_ref[:, left], high_ref[...])
        total = total + product(high_ref[:, left], low_ref[...])
        total = total + product(low_ref[:, left], high_ref[...])
        sum_ref[...] += total
        sum_ref[:, left] += product(low_ref[:, left], low_ref[:, left])
        return 0

    lax.fori_loop(0, steps, step, 0)
    if last:
        far = lag_count - 2
        for j in range(far):
            out_ref[j * NODES : (j + 1) * NODES, :] = sum_ref[:NODES, j * NODES : (j + 1) * NODES]
            place = (far + j) * NODES
            out_ref[place : place + NODES, :] = sum_ref[NODES:, (j + 1) * NODES : (j + 2) * NODES]
        which = jnp.where(4 * chan_ref[0] >= total_lags, 1, 0)
        row = pl.multiple_of(which * NODES, NODES)
        column = pl.multiple_of((far + which) * NODES, NODES)
        out_ref[2 * far * NODES :, :] = sum_ref[pl.ds(row, NODES), pl.ds(column, NODES)]
    else:
        out_ref[...] = sum_ref[...]


def gram_part(chan, lags, mine, other, carried, after, earlier):
    first, last = carried is None, after is not None
    count = lags.shape[0] // 2 + 2
    blocks = 2 * (count - 2) + 1
    operands = [chan, lags, mine, other]
    if not first:
        operands += list(carried)
    if last:
        operands.append(after)
    if last:
        out_shape = jax.ShapeDtypeStruct((blocks * NODES, NODES), jnp.float32)
    else:
        out_shape = (
            jax.ShapeDtypeStruct((2 * NODES, count * NODES), jnp.float32),
            jax.ShapeDtypeStruct((MAXLAG, NODES), jnp.float32),
        )
    rows = 2 * mine.shape[0] + (0 if first else MAXLAG) + (MAXLAG if last else 0)
    vmem = pl.BlockSpec(memory_space=pltpu.VMEM)
    smem = pl.BlockSpec(memory_space=pltpu.SMEM)
    step_rows = 512
    return pl.pallas_call(
        functools.partial(gram_kernel, first, last, len(earlier)),
        out_shape=out_shape,
        in_specs=[smem, smem] + [vmem] * (len(operands) - 2) + [pl.BlockSpec(memory_space=pl.ANY)] * len(earlier),
        out_specs=vmem if last else (vmem, vmem),
        scratch_shapes=[
            pltpu.VMEM((rows, NODES), jnp.float32),
            pltpu.VMEM((step_rows, count * NODES), jnp.bfloat16),
            pltpu.VMEM((step_rows, count * NODES), jnp.bfloat16),
            pltpu.VMEM((2 * NODES, count * NODES), jnp.float32),
        ],
        compiler_params=pltpu.CompilerParams(vmem_limit_bytes=12 << 20),
    )(*operands, *earlier)


def row_of(value, index):
    return jnp.broadcast_to(value[index : index + 1, :], value.shape)


def column_of(value, index):
    return jnp.broadcast_to(value[:, index : index + 1], value.shape)


def factor_block(block):
    count = len(block)
    sub = lax.broadcasted_iota(jnp.int32, (GROUP, BLOCK), 0)
    lane = lax.broadcasted_iota(jnp.int32, (GROUP, BLOCK), 1)
    state = list(block)
    result = [None] * count
    full = [None] * count
    columns = [column_of(state[0], m) for m in range(GROUP)]
    for g in range(count):
        first_lane, next_lane = GROUP * g, GROUP * (g + 1)
        here = (lane >= first_lane) & (lane < next_lane)
        span = g // SPAN
        more = g + 1 < count
        if more:
            next_columns = [column_of(state[g + 1], next_lane + m) for m in range(GROUP)]
            next_left = [column_of(state[g + 1], first_lane + m) for m in range(GROUP)]
            state[g + 1] = jnp.where(here, 0.0, state[g + 1])
        top = jnp.where(here, jnp.where(lane == sub + first_lane, 1.0, 0.0), state[g])
        diagonal = jnp.zeros_like(top)
        scale, factors, rows = [], {}, []
        pivots = [row_of(columns[m], m) for m in range(GROUP)]
        for m in range(GROUP):
            pivot = pivots[m]
            scale.append(lax.rsqrt(pivot))
            left = columns[m] * scale[m]
            for n in range(m + 1, GROUP):
                factors[m, n] = row_of(columns[m], n) * scale[m]
                pivots[n] = pivots[n] - factors[m, n] * factors[m, n]
                columns[n] = columns[n] - left * factors[m, n]
            if more:
                next_left[m] = next_left[m] * scale[m]
                for n in range(m + 1, GROUP):
                    next_left[n] = next_left[n] - next_left[m] * factors[m, n]
                for n in range(GROUP):
                    next_columns[n] = next_columns[n] - next_left[m] * row_of(next_left[m], n)
            rows.append(row_of(top, m) * scale[m])
            below = jnp.where(sub > m, left, 0.0)
            top = jnp.where(sub == m, rows[m], top - below * rows[m])
            entries = pivot * scale[m]
            for n in range(m + 1, GROUP):
                entries = jnp.where(lane == first_lane + n, factors[m, n], entries)
            diagonal = jnp.where(sub == m, entries, diagonal)
            if more:
                state[g + 1] = state[g + 1] - next_left[m] * rows[m]
        full[g] = top
        result[g] = jnp.where(lane >= next_lane, top, jnp.where(lane >= sub + first_lane, diagonal, 0.0))
        state[g] = jnp.where(lane < next_lane, top, 0.0)
        columns = next_columns
        for s in range(g + 2, min(count, (span + 2) * SPAN)):
            left = [column_of(state[s], first_lane + m) for m in range(GROUP)]
            value = jnp.where(here, 0.0, state[s])
            for m in range(GROUP):
                left[m] = left[m] * scale[m]
                for n in range(m + 1, GROUP):
                    left[n] = left[n] - left[m] * factors[m, n]
                value = value - left[m] * rows[m]
            state[s] = value
        rest = (span + 2) * SPAN
        if g % SPAN == SPAN - 1 and rest < count:
            begin = span * SPAN
            left = jnp.concatenate(full[begin : g + 1], axis=0)
            right = [
                jnp.where((lane >= GROUP * (i + 1)) & (lane < next_lane), 0.0, full[i]) for i in range(begin, g + 1)
            ]
            update = lax.dot_general(
                left[:, GROUP * rest :],
                jnp.concatenate(right, axis=0),
                CONTRACT_ROWS,
                precision=HIGHEST,
                preferred_element_type=jnp.float32,
            )
            inside = (lane >= GROUP * begin) & (lane < next_lane)
            for s in range(rest, count):
                place = GROUP * (s - rest)
                state[s] = jnp.where(inside, 0.0, state[s]) - update[place : place + GROUP]
    return result, state


def arrange(scale, layout, half_ref, mine_refs, other_refs, natural_ref, ordered_ref):
    chan_count = 4
    lag_count = 2 * chan_count
    far = lag_count // 2
    width = NODES // chan_count

    def rows_of(refs, high, start, stop):
        found, base = [], 0
        for ref, pieces in zip(refs, layout):
            for first, count, place in pieces[high]:
                low, end = max(start, base + first), min(stop, base + first + count)
                if low < end:
                    offset = place - base - first
                    found.append(ref[low + offset : end + offset, :])
            base += ref.shape[0] // 2
        return found[0] if len(found) == 1 else jnp.concatenate(found, axis=0)

    def place(refs, low):
        for high in range(2):
            chan = 2 * high + low
            pairs = [(2 * chan + i, (2 * chan + i + d) % lag_count) for i in range(2) for d in range(far)]
            odd = 2 * chan // far
            pairs.append((2 * chan + odd, (2 * chan + odd + far) % lag_count))
            for index, (left, right) in enumerate(pairs):
                block = rows_of(refs, high, index * NODES, (index + 1) * NODES)
                natural_ref[left * NODES : (left + 1) * NODES, right * NODES : (right + 1) * NODES] = block
                if left != right:
                    natural_ref[right * NODES : (right + 1) * NODES, left * NODES : (left + 1) * NODES] = block.T

    for low in range(2):

        @pl.when(half_ref[0] == low)
        def _():
            place(mine_refs, low)
            place(other_refs, 1 - low)

    lane_part = lax.broadcasted_iota(jnp.int32, (width, NODES), 1) // width

    def rows_of_lag(lag, _):
        for group in range(chan_count):
            source = pl.ds(pl.multiple_of(lag * NODES + group * width, width), width)
            target = pl.ds(pl.multiple_of(group * lag_count * width + lag * width, width), width)
            for half in range(2):
                parts = [natural_ref[source, (4 * half + i) * NODES : (4 * half + i + 1) * NODES] for i in range(4)]
                turned = []
                for shift in range(4):
                    value = parts[shift]
                    for lane in range(1, 4):
                        value = jnp.where(lane_part == lane, parts[(lane + shift) % 4], value)
                    turned.append(pltpu.roll(value, shift * width, 1) if shift else value)
                for other in range(group, chan_count):
                    block = turned[-other % 4]
                    for i in range(1, 4):
                        block = jnp.where(lane_part == i, turned[(i - other) % 4], block)
                    column = (2 * other + half) * BLOCK
                    ordered_ref[target, column : column + BLOCK] = block * scale
        return 0

    lax.fori_loop(0, lag_count, rows_of_lag, 0)


def cholesky_kernel(scale, layout, half_ref, *refs):
    parts = len(layout)
    mine_refs, other_refs = refs[:parts], refs[parts : 2 * parts]
    out_ref, natural_ref, ordered_ref, result_ref, panel_ref, inverse_ref, sent = refs[2 * parts :]
    arrange(scale, layout, half_ref, mine_refs, other_refs, natural_ref, ordered_ref)
    count = out_ref.shape[0] // BLOCK
    result_ref[...] = jnp.zeros_like(result_ref)
    panel_ref[...] = ordered_ref[:BLOCK, :]

    def send(k):
        rows = pl.ds(pl.multiple_of(k * BLOCK, BLOCK), BLOCK)
        return pltpu.make_async_copy(result_ref.at[rows, :], out_ref.at[rows, :], sent.at[k])

    def step(k, _):
        start = pl.multiple_of(k * BLOCK, BLOCK)
        block = [panel_ref[GROUP * s : GROUP * (s + 1), pl.ds(start, BLOCK)] for s in range(BLOCK // GROUP)]
        block, inverse = factor_block(block)
        for s in range(BLOCK // GROUP):
            result_ref[pl.ds(pl.multiple_of(start + GROUP * s, GROUP), GROUP), pl.ds(start, BLOCK)] = block[s]
            inverse_ref[GROUP * s : GROUP * (s + 1), :] = inverse[s]
        for kk in range(count - 1):

            @pl.when(k == kk)
            def _():
                now, later = kk * BLOCK, (kk + 1) * BLOCK
                row = jnp.dot(
                    inverse_ref[...], panel_ref[:, later:], precision=HIGHEST, preferred_element_type=jnp.float32
                )

                def product(left, right):
                    return lax.dot_general(
                        left, right, CONTRACT_ROWS, precision=HIGHEST, preferred_element_type=jnp.float32
                    )

                panel = ordered_ref[later : later + BLOCK, later:]
                if kk:
                    panel = panel - product(result_ref[:now, later : later + BLOCK], result_ref[:now, later:])
                result_ref[now:later, later:] = row
                panel_ref[:, later:] = panel - product(row[:, :BLOCK], row)

        send(k).start()
        return 0

    lax.fori_loop(0, count, step, 0)
    for k in range(count):
        send(k).wait()


def cholesky(half, mine, other, layout, size, scale):
    vmem = pl.BlockSpec(memory_space=pltpu.VMEM)
    return pl.pallas_call(
        functools.partial(cholesky_kernel, scale, layout),
        out_shape=jax.ShapeDtypeStruct((size, size), jnp.float32),
        in_specs=[pl.BlockSpec(memory_space=pltpu.SMEM)] + [vmem] * (2 * len(mine)),
        out_specs=pl.BlockSpec(memory_space=pl.ANY),
        scratch_shapes=[
            pltpu.VMEM((size, size), jnp.float32),
            pltpu.VMEM((size, size), jnp.float32),
            pltpu.VMEM((size, size), jnp.float32),
            pltpu.VMEM((BLOCK, size), jnp.float32),
            pltpu.VMEM((BLOCK, BLOCK), jnp.float32),
            pltpu.SemaphoreType.DMA((size // BLOCK,)),
        ],
        compiler_params=pltpu.CompilerParams(vmem_limit_bytes=24 << 20),
    )(half, *mine, *other)


def on_device(signals, channel_node, lag_offsets):
    chan = lax.axis_index("chan").reshape(1)
    half = chan % 2
    send = project(signals, channel_node, 1 - half)
    received = swap(send, "chan", 1)
    keep = project(signals, channel_node, half)
    sizes = chunk_sizes(signals.shape[0])
    totals = add_parts(keep, received, [size // 2 for size in sizes])
    sent = [swap(total, "chan", 2) for total in totals]
    carried = after = None
    for index in range(len(sizes)):
        first, last = index == 0, index == len(sizes) - 1
        value = add(totals[index], sent[index], *(() if first else (carried[1], after)))
        other = swap(value, "chan", 1)
        if first:
            head = jnp.where(half[0] == 0, value[:MAXLAG], other[:MAXLAG])
            after = first_rows_of_next(head)
        earlier = (head,) if first else ()
        carried = gram_part(chan, lag_offsets, value, other, carried, after if last else None, earlier)
    rows = carried.shape[0] // 2
    mine = [route.reduce(part) for route, part in zip(routes(), (carried[:rows], carried[rows:]))]
    other = [swap(value, "chan", 1) for value in mine]
    layout = [[route.pieces(rows, high) for high in range(2)] for route in routes()]
    size = lag_offsets.shape[0] * NODES
    return cholesky(half, mine, other, layout, size, 1.0 / (signals.shape[0] * lax.axis_size("tm")))


def solution(mesh):
    return jax.shard_map(
        on_device, mesh=mesh, in_specs=(P("tm", "chan"), P("chan"), P()), out_specs=P(), check_vma=False
    )
```

```python
import functools
import math

import jax
import jax.numpy as jnp
from jax import lax
from jax.experimental import pallas as pl
from jax.experimental.pallas import tpu as pltpu
from jax.sharding import PartitionSpec as P

NODES = 128
CH = 2048
MAXLAG = 512
BLOCK = 128
GROUP = 8
SPAN = 4
CHUNK_QUARTERS = (1, 1)
HIGHEST = lax.Precision.HIGHEST
CONTRACT_ROWS = (((0,), (0,)), ((), ()))


def swap(value, axis, bit):
    count = lax.axis_size(axis)
    return lax.ppermute(value, axis, [(i, i ^ bit) for i in range(count)])


def bits_of(axis):
    count = lax.axis_size(axis)
    return [1 << i for i in range(count.bit_length() - 1)]


def halve(value, axis, bit):
    half = value.shape[0] // 2
    mine = (lax.axis_index(axis) // bit) % 2
    send = lax.dynamic_slice_in_dim(value, (1 - mine) * half, half, 0)
    keep = lax.dynamic_slice_in_dim(value, mine * half, half, 0)
    return keep + swap(send, axis, bit)


def double(value, axis, bit):
    mine = (lax.axis_index(axis) // bit) % 2
    other = swap(value, axis, bit)
    low = jnp.where(mine == 0, value, other)
    high = jnp.where(mine == 0, other, value)
    return jnp.concatenate([low, high], axis=0)


class Route:
    def __init__(self, scatter, whole, gather):
        self.scatter, self.whole, self.gather = scatter, whole, gather

    def reduce(self, value):
        for bit in self.scatter:
            value = halve(value, "tm", bit)
        for bit in self.whole:
            value = value + swap(value, "tm", bit)
        for axis, bit in self.gather:
            value = double(value, axis, bit)
        return value

    def pieces(self, rows, high):
        unit = rows >> len(self.scatter)
        found = []
        for index in range(1 << len(self.scatter)):
            value = {("chan", 2): high}
            for i, bit in enumerate(self.scatter):
                value["tm", bit] = index >> (len(self.scatter) - 1 - i) & 1
            place = sum(value[stage] << i for i, stage in enumerate(self.gather))
            found.append((index * unit, unit, place * unit))
        return found


def routes():
    bits = bits_of("tm")
    upper = ("chan", 2)
    ahead, last = bits[:-1], bits[-1:]
    first = Route(ahead, last, [("tm", bit) for bit in ahead[::-1]] + [upper])
    turned = ahead[1:] + ahead[:1]
    second = Route(turned, last, [("tm", bit) for bit in turned[:0:-1]] + [upper] + [("tm", turned[0])])
    return first, second


def add_kernel(left_ref, right_ref, *refs):
    refs[-1][...] = left_ref[...] + right_ref[...]


def add(left, right, *earlier):
    vmem = pl.BlockSpec(memory_space=pltpu.VMEM)
    return pl.pallas_call(
        add_kernel,
        out_shape=jax.ShapeDtypeStruct(left.shape, left.dtype),
        in_specs=[vmem, vmem] + [pl.BlockSpec(memory_space=pl.ANY)] * len(earlier),
        out_specs=vmem,
        compiler_params=pltpu.CompilerParams(vmem_limit_bytes=8 << 20),
    )(left, right, *earlier)


def add_parts_kernel(left_ref, right_ref, *out_refs):
    start = 0
    for out_ref in out_refs:
        here = slice(start, start + out_ref.shape[0])
        out_ref[...] = left_ref[here, :] + right_ref[here, :]
        start += out_ref.shape[0]


def add_parts(left, right, sizes):
    vmem = pl.BlockSpec(memory_space=pltpu.VMEM)
    return pl.pallas_call(
        add_parts_kernel,
        out_shape=tuple(jax.ShapeDtypeStruct((size, left.shape[1]), left.dtype) for size in sizes),
        in_specs=[vmem, vmem],
        out_specs=(vmem,) * len(sizes),
        compiler_params=pltpu.CompilerParams(vmem_limit_bytes=8 << 20),
    )(left, right)


def first_rows_of_next(rows):
    count = lax.axis_size("tm")
    return lax.ppermute(rows, "tm", [(i, i - 1) for i in range(1, count)])


def project_kernel(half_ref, nodes_ref, signals_ref, out_ref, onehot_ref):
    @pl.when(pl.program_id(0) == 0)
    def _():
        node = lax.broadcasted_iota(jnp.int32, onehot_ref.shape, 0).astype(jnp.float32)
        scale = 1.0 / math.sqrt(CH // NODES)
        onehot_ref[...] = jnp.where(node == nodes_ref[...], scale, 0.0).astype(jnp.bfloat16)

    out_ref[...] = lax.dot_general(
        signals_ref[...], onehot_ref[...], (((1,), (1,)), ((), ())), preferred_element_type=jnp.float32
    )


def chunk_sizes(rows):
    return [rows * quarters // sum(CHUNK_QUARTERS) for quarters in CHUNK_QUARTERS]


def project(signals, channel_nodes, half):
    rows, channels = signals.shape
    parts = [size // 2 for size in chunk_sizes(rows)]
    step = math.gcd(512, *parts)
    steps = sum(parts) // step

    def block_of(i, half):
        done, block = 0, i
        for part in parts:
            count = part // step
            block = jnp.where(i >= done, done + i + half[0] * count, block)
            done += count
        return block, 0

    grid_spec = pltpu.PrefetchScalarGridSpec(
        num_scalar_prefetch=1,
        grid=(steps,),
        in_specs=[
            pl.BlockSpec((1, channels), lambda i, half: (0, 0)),
            pl.BlockSpec((step, channels), block_of),
        ],
        out_specs=pl.BlockSpec((step, NODES), lambda i, half: (i, 0)),
        scratch_shapes=[pltpu.VMEM((NODES, channels), jnp.bfloat16)],
    )
    return pl.pallas_call(
        project_kernel,
        out_shape=jax.ShapeDtypeStruct((rows // 2, NODES), jnp.float32),
        grid_spec=grid_spec,
        compiler_params=pltpu.CompilerParams(vmem_limit_bytes=8 << 20),
    )(half, channel_nodes, signals)


def gram_kernel(stage, earlier, chan_ref, all_lags_ref, *refs):
    refs = list(refs)
    mine_ref = refs.pop(0)
    other_ref = None if stage == "own" else refs.pop(0)
    sum_in_ref, tail_ref, after_ref = (None,) * 3 if stage == "first" else [refs.pop(0) for _ in range(3)]
    del refs[:earlier]
    out_ref = refs.pop(0)
    tail_out_ref = refs.pop(0) if stage == "first" else None
    ext_ref, high_ref, low_ref, sum_ref = refs
    half = mine_ref.shape[0]
    total_lags = all_lags_ref.shape[0]
    lag_count = sum_ref.shape[1] // NODES
    lags = [all_lags_ref[lax.rem(2 * chan_ref[0] + i, total_lags)] for i in range(lag_count)]
    own_half = lax.rem(chan_ref[0], 2)
    step_rows = high_ref.shape[0]

    def rows_from(start, count):
        return pl.ds(pl.multiple_of(start, math.gcd(MAXLAG, half)), count)

    if stage == "own":
        ext_ref[rows_from((1 - own_half) * MAXLAG, half), :] = mine_ref[...]
        ext_ref[rows_from(own_half * half, MAXLAG), :] = jnp.where(own_half == 0, tail_ref[...], after_ref[...])
        begin, steps = 0, half // step_rows
    else:
        lead = 0 if stage == "first" else MAXLAG
        end = lead + 2 * half
        ext_ref[rows_from(lead + own_half * half, half), :] = mine_ref[...]
        ext_ref[rows_from(lead + (1 - own_half) * half, half), :] = other_ref[...]
        if stage == "first":
            tail_out_ref[...] = ext_ref[end - MAXLAG : end, :]
            begin, steps = 0, (end - MAXLAG) // step_rows
        else:
            ext_ref[:lead, :] = tail_ref[...]
            ext_ref[end:, :] = after_ref[...]
            begin, steps = (1 - own_half) * half, (end - half) // step_rows
    sum_ref[...] = jnp.zeros_like(sum_ref) if stage == "first" else sum_in_ref[...]
    part = 128

    def step(i, _):
        start = begin + i * step_rows
        for lag in range(lag_count):
            for row in range(0, step_rows, part):
                value = ext_ref[pl.ds(start + row + lags[lag], part), :]
                high = value.astype(jnp.bfloat16)
                high_ref[row : row + part, lag * NODES : (lag + 1) * NODES] = high
                low_ref[row : row + part, lag * NODES : (lag + 1) * NODES] = (
                    value - high.astype(jnp.float32)
                ).astype(jnp.bfloat16)

        def product(left, right):
            return lax.dot_general(left, right, CONTRACT_ROWS, preferred_element_type=jnp.float32)

        left = slice(0, 2 * NODES)
        total = product(high_ref[:, left], high_ref[...])
        total = total + product(high_ref[:, left], low_ref[...])
        total = total + product(low_ref[:, left], high_ref[...])
        sum_ref[...] += total
        sum_ref[:, left] += product(low_ref[:, left], low_ref[:, left])
        return 0

    lax.fori_loop(0, steps, step, 0)
    if stage == "rest":
        far = lag_count - 2
        for j in range(far):
            out_ref[j * NODES : (j + 1) * NODES, :] = sum_ref[:NODES, j * NODES : (j + 1) * NODES]
            place = (far + j) * NODES
            out_ref[place : place + NODES, :] = sum_ref[NODES:, (j + 1) * NODES : (j + 2) * NODES]
        which = jnp.where(4 * chan_ref[0] >= total_lags, 1, 0)
        row = pl.multiple_of(which * NODES, NODES)
        column = pl.multiple_of((far + which) * NODES, NODES)
        out_ref[2 * far * NODES :, :] = sum_ref[pl.ds(row, NODES), pl.ds(column, NODES)]
    else:
        out_ref[...] = sum_ref[...]


def gram_part(stage, chan, lags, values, carried=(), earlier=()):
    count = lags.shape[0] // 2 + 2
    half = values[0].shape[0]
    sums = jax.ShapeDtypeStruct((2 * NODES, count * NODES), jnp.float32)
    vmem = pl.BlockSpec(memory_space=pltpu.VMEM)
    smem = pl.BlockSpec(memory_space=pltpu.SMEM)
    if stage == "first":
        rows = 2 * half
        out_shape, out_specs = (sums, jax.ShapeDtypeStruct((MAXLAG, NODES), jnp.float32)), (vmem, vmem)
    elif stage == "own":
        rows = half + MAXLAG
        out_shape, out_specs = sums, vmem
    else:
        rows = 2 * half + 2 * MAXLAG
        out_shape, out_specs = jax.ShapeDtypeStruct(((2 * count - 3) * NODES, NODES), jnp.float32), vmem
    step_rows = 512
    return pl.pallas_call(
        functools.partial(gram_kernel, stage, len(earlier)),
        out_shape=out_shape,
        in_specs=[smem, smem]
        + [vmem] * (len(values) + len(carried))
        + [pl.BlockSpec(memory_space=pl.ANY)] * len(earlier),
        out_specs=out_specs,
        scratch_shapes=[
            pltpu.VMEM((rows, NODES), jnp.float32),
            pltpu.VMEM((step_rows, count * NODES), jnp.bfloat16),
            pltpu.VMEM((step_rows, count * NODES), jnp.bfloat16),
            pltpu.VMEM((2 * NODES, count * NODES), jnp.float32),
        ],
        compiler_params=pltpu.CompilerParams(vmem_limit_bytes=12 << 20),
    )(chan, lags, *values, *carried, *earlier)


def row_of(value, index):
    return jnp.broadcast_to(value[index : index + 1, :], value.shape)


def column_of(value, index):
    return jnp.broadcast_to(value[:, index : index + 1], value.shape)


def factor_block(block):
    count = len(block)
    sub = lax.broadcasted_iota(jnp.int32, (GROUP, BLOCK), 0)
    lane = lax.broadcasted_iota(jnp.int32, (GROUP, BLOCK), 1)
    state = list(block)
    result = [None] * count
    full = [None] * count
    columns = [column_of(state[0], m) for m in range(GROUP)]
    for g in range(count):
        first_lane, next_lane = GROUP * g, GROUP * (g + 1)
        here = (lane >= first_lane) & (lane < next_lane)
        span = g // SPAN
        more = g + 1 < count
        if more:
            next_columns = [column_of(state[g + 1], next_lane + m) for m in range(GROUP)]
            next_left = [column_of(state[g + 1], first_lane + m) for m in range(GROUP)]
            state[g + 1] = jnp.where(here, 0.0, state[g + 1])
        top = jnp.where(here, jnp.where(lane == sub + first_lane, 1.0, 0.0), state[g])
        diagonal = jnp.zeros_like(top)
        scale, factors, rows = [], {}, []
        pivots = [row_of(columns[m], m) for m in range(GROUP)]
        for m in range(GROUP):
            pivot = pivots[m]
            scale.append(lax.rsqrt(pivot))
            left = columns[m] * scale[m]
            for n in range(m + 1, GROUP):
                factors[m, n] = row_of(columns[m], n) * scale[m]
                pivots[n] = pivots[n] - factors[m, n] * factors[m, n]
                columns[n] = columns[n] - left * factors[m, n]
            if more:
                next_left[m] = next_left[m] * scale[m]
                for n in range(m + 1, GROUP):
                    next_left[n] = next_left[n] - next_left[m] * factors[m, n]
                for n in range(GROUP):
                    next_columns[n] = next_columns[n] - next_left[m] * row_of(next_left[m], n)
            rows.append(row_of(top, m) * scale[m])
            below = jnp.where(sub > m, left, 0.0)
            top = jnp.where(sub == m, rows[m], top - below * rows[m])
            entries = pivot * scale[m]
            for n in range(m + 1, GROUP):
                entries = jnp.where(lane == first_lane + n, factors[m, n], entries)
            diagonal = jnp.where(sub == m, entries, diagonal)
            if more:
                state[g + 1] = state[g + 1] - next_left[m] * rows[m]
        full[g] = top
        result[g] = jnp.where(lane >= next_lane, top, jnp.where(lane >= sub + first_lane, diagonal, 0.0))
        state[g] = jnp.where(lane < next_lane, top, 0.0)
        columns = next_columns
        for s in range(g + 2, min(count, (span + 2) * SPAN)):
            left = [column_of(state[s], first_lane + m) for m in range(GROUP)]
            value = jnp.where(here, 0.0, state[s])
            for m in range(GROUP):
                left[m] = left[m] * scale[m]
                for n in range(m + 1, GROUP):
                    left[n] = left[n] - left[m] * factors[m, n]
                value = value - left[m] * rows[m]
            state[s] = value
        rest = (span + 2) * SPAN
        if g % SPAN == SPAN - 1 and rest < count:
            begin = span * SPAN
            left = jnp.concatenate(full[begin : g + 1], axis=0)
            right = [
                jnp.where((lane >= GROUP * (i + 1)) & (lane < next_lane), 0.0, full[i]) for i in range(begin, g + 1)
            ]
            update = lax.dot_general(
                left[:, GROUP * rest :],
                jnp.concatenate(right, axis=0),
                CONTRACT_ROWS,
                precision=HIGHEST,
                preferred_element_type=jnp.float32,
            )
            inside = (lane >= GROUP * begin) & (lane < next_lane)
            for s in range(rest, count):
                place = GROUP * (s - rest)
                state[s] = jnp.where(inside, 0.0, state[s]) - update[place : place + GROUP]
    return result, state


def arrange(scale, layout, half_ref, mine_refs, other_refs, natural_ref, ordered_ref):
    chan_count = 4
    lag_count = 2 * chan_count
    far = lag_count // 2
    width = NODES // chan_count

    def rows_of(refs, high, start, stop):
        found, base = [], 0
        for ref, pieces in zip(refs, layout):
            for first, count, place in pieces[high]:
                low, end = max(start, base + first), min(stop, base + first + count)
                if low < end:
                    offset = place - base - first
                    found.append(ref[low + offset : end + offset, :])
            base += ref.shape[0] // 2
        return found[0] if len(found) == 1 else jnp.concatenate(found, axis=0)

    def place(refs, low):
        for high in range(2):
            chan = 2 * high + low
            pairs = [(2 * chan + i, (2 * chan + i + d) % lag_count) for i in range(2) for d in range(far)]
            odd = 2 * chan // far
            pairs.append((2 * chan + odd, (2 * chan + odd + far) % lag_count))
            for index, (left, right) in enumerate(pairs):
                block = rows_of(refs, high, index * NODES, (index + 1) * NODES)
                natural_ref[left * NODES : (left + 1) * NODES, right * NODES : (right + 1) * NODES] = block
                if left != right:
                    natural_ref[right * NODES : (right + 1) * NODES, left * NODES : (left + 1) * NODES] = block.T

    for low in range(2):

        @pl.when(half_ref[0] == low)
        def _():
            place(mine_refs, low)
            place(other_refs, 1 - low)

    lane_part = lax.broadcasted_iota(jnp.int32, (width, NODES), 1) // width

    def rows_of_lag(lag, _):
        for group in range(chan_count):
            source = pl.ds(pl.multiple_of(lag * NODES + group * width, width), width)
            target = pl.ds(pl.multiple_of(group * lag_count * width + lag * width, width), width)
            for half in range(2):
                parts = [natural_ref[source, (4 * half + i) * NODES : (4 * half + i + 1) * NODES] for i in range(4)]
                turned = []
                for shift in range(4):
                    value = parts[shift]
                    for lane in range(1, 4):
                        value = jnp.where(lane_part == lane, parts[(lane + shift) % 4], value)
                    turned.append(pltpu.roll(value, shift * width, 1) if shift else value)
                for other in range(group, chan_count):
                    block = turned[-other % 4]
                    for i in range(1, 4):
                        block = jnp.where(lane_part == i, turned[(i - other) % 4], block)
                    column = (2 * other + half) * BLOCK
                    ordered_ref[target, column : column + BLOCK] = block * scale
        return 0

    lax.fori_loop(0, lag_count, rows_of_lag, 0)


def cholesky_kernel(scale, layout, half_ref, *refs):
    parts = len(layout)
    mine_refs, other_refs = refs[:parts], refs[parts : 2 * parts]
    out_ref, natural_ref, ordered_ref, result_ref, panel_ref, inverse_ref, sent = refs[2 * parts :]
    arrange(scale, layout, half_ref, mine_refs, other_refs, natural_ref, ordered_ref)
    count = out_ref.shape[0] // BLOCK
    result_ref[...] = jnp.zeros_like(result_ref)
    panel_ref[...] = ordered_ref[:BLOCK, :]

    def send(k):
        rows = pl.ds(pl.multiple_of(k * BLOCK, BLOCK), BLOCK)
        return pltpu.make_async_copy(result_ref.at[rows, :], out_ref.at[rows, :], sent.at[k])

    def step(k, _):
        start = pl.multiple_of(k * BLOCK, BLOCK)
        block = [panel_ref[GROUP * s : GROUP * (s + 1), pl.ds(start, BLOCK)] for s in range(BLOCK // GROUP)]
        block, inverse = factor_block(block)
        for s in range(BLOCK // GROUP):
            result_ref[pl.ds(pl.multiple_of(start + GROUP * s, GROUP), GROUP), pl.ds(start, BLOCK)] = block[s]
            inverse_ref[GROUP * s : GROUP * (s + 1), :] = inverse[s]
        for kk in range(count - 1):

            @pl.when(k == kk)
            def _():
                now, later = kk * BLOCK, (kk + 1) * BLOCK
                row = jnp.dot(
                    inverse_ref[...], panel_ref[:, later:], precision=HIGHEST, preferred_element_type=jnp.float32
                )

                def product(left, right):
                    return lax.dot_general(
                        left, right, CONTRACT_ROWS, precision=HIGHEST, preferred_element_type=jnp.float32
                    )

                panel = ordered_ref[later : later + BLOCK, later:]
                if kk:
                    panel = panel - product(result_ref[:now, later : later + BLOCK], result_ref[:now, later:])
                result_ref[now:later, later:] = row
                panel_ref[:, later:] = panel - product(row[:, :BLOCK], row)

        send(k).start()
        return 0

    lax.fori_loop(0, count, step, 0)
    for k in range(count):
        send(k).wait()


def cholesky(half, mine, other, layout, size, scale):
    vmem = pl.BlockSpec(memory_space=pltpu.VMEM)
    return pl.pallas_call(
        functools.partial(cholesky_kernel, scale, layout),
        out_shape=jax.ShapeDtypeStruct((size, size), jnp.float32),
        in_specs=[pl.BlockSpec(memory_space=pltpu.SMEM)] + [vmem] * (2 * len(mine)),
        out_specs=pl.BlockSpec(memory_space=pl.ANY),
        scratch_shapes=[
            pltpu.VMEM((size, size), jnp.float32),
            pltpu.VMEM((size, size), jnp.float32),
            pltpu.VMEM((size, size), jnp.float32),
            pltpu.VMEM((BLOCK, size), jnp.float32),
            pltpu.VMEM((BLOCK, BLOCK), jnp.float32),
            pltpu.SemaphoreType.DMA((size // BLOCK,)),
        ],
        compiler_params=pltpu.CompilerParams(vmem_limit_bytes=24 << 20),
    )(half, *mine, *other)


def on_device(signals, channel_node, lag_offsets):
    chan = lax.axis_index("chan").reshape(1)
    half = chan % 2
    channel_nodes = channel_node.astype(jnp.float32).reshape(1, -1)
    send = project(signals, channel_nodes, 1 - half)
    received = swap(send, "chan", 1)
    keep = project(signals, channel_nodes, half)
    sizes = chunk_sizes(signals.shape[0])
    totals = add_parts(keep, received, [size // 2 for size in sizes])
    sent = [swap(total, "chan", 2) for total in totals]
    value = add(totals[0], sent[0])
    other = swap(value, "chan", 1)
    head = jnp.where(half[0] == 0, value[:MAXLAG], other[:MAXLAG])
    after = first_rows_of_next(head)
    sums, tail = gram_part("first", chan, lag_offsets, (value, other), earlier=(head,))
    value = add(totals[1], sent[1], tail, after)
    other = swap(value, "chan", 1)
    sums = gram_part("own", chan, lag_offsets, (value,), (sums, tail, after))
    carried = gram_part("rest", chan, lag_offsets, (value, other), (sums, tail, after))
    rows = carried.shape[0] // 2
    mine = [route.reduce(part) for route, part in zip(routes(), (carried[:rows], carried[rows:]))]
    other = [swap(value, "chan", 1) for value in mine]
    layout = [[route.pieces(rows, high) for high in range(2)] for route in routes()]
    size = lag_offsets.shape[0] * NODES
    return cholesky(half, mine, other, layout, size, 1.0 / (signals.shape[0] * lax.axis_size("tm")))


def solution(mesh):
    return jax.shard_map(
        on_device, mesh=mesh, in_specs=(P("tm", "chan"), P("chan"), P()), out_specs=P(), check_vma=False
    )
```

```python
import functools
import math

import jax
import jax.numpy as jnp
from jax import lax
from jax.experimental import pallas as pl
from jax.experimental.pallas import tpu as pltpu
from jax.sharding import PartitionSpec as P

NODES = 128
CH = 2048
MAXLAG = 512
BLOCK = 128
GROUP = 8
SPAN = 4
CHUNK_QUARTERS = (1, 3)
HIGHEST = lax.Precision.HIGHEST
CONTRACT_ROWS = (((0,), (0,)), ((), ()))


def swap(value, axis, bit):
    count = lax.axis_size(axis)
    return lax.ppermute(value, axis, [(i, i ^ bit) for i in range(count)])


def bits_of(axis):
    count = lax.axis_size(axis)
    return [1 << i for i in range(count.bit_length() - 1)]


def halve(value, axis, bit):
    half = value.shape[0] // 2
    mine = (lax.axis_index(axis) // bit) % 2
    send = lax.dynamic_slice_in_dim(value, (1 - mine) * half, half, 0)
    keep = lax.dynamic_slice_in_dim(value, mine * half, half, 0)
    return keep + swap(send, axis, bit)


def double(value, axis, bit):
    mine = (lax.axis_index(axis) // bit) % 2
    other = swap(value, axis, bit)
    low = jnp.where(mine == 0, value, other)
    high = jnp.where(mine == 0, other, value)
    return jnp.concatenate([low, high], axis=0)


class Route:
    def __init__(self, scatter, whole, gather):
        self.scatter, self.whole, self.gather = scatter, whole, gather

    def reduce(self, value):
        for bit in self.scatter:
            value = halve(value, "tm", bit)
        for bit in self.whole:
            value = value + swap(value, "tm", bit)
        for axis, bit in self.gather:
            value = double(value, axis, bit)
        return value

    def pieces(self, rows, high):
        unit = rows >> len(self.scatter)
        found = []
        for index in range(1 << len(self.scatter)):
            value = {("chan", 2): high}
            for i, bit in enumerate(self.scatter):
                value["tm", bit] = index >> (len(self.scatter) - 1 - i) & 1
            place = sum(value[stage] << i for i, stage in enumerate(self.gather))
            found.append((index * unit, unit, place * unit))
        return found


def routes():
    bits = bits_of("tm")
    upper = ("chan", 2)
    ahead, last = bits[:-1], bits[-1:]
    first = Route(ahead, last, [("tm", bit) for bit in ahead[::-1]] + [upper])
    turned = ahead[1:] + ahead[:1]
    second = Route(turned, last, [("tm", bit) for bit in turned[:0:-1]] + [upper] + [("tm", turned[0])])
    return first, second


def add_kernel(left_ref, right_ref, *refs):
    refs[-1][...] = left_ref[...] + right_ref[...]


def add(left, right, *earlier):
    vmem = pl.BlockSpec(memory_space=pltpu.VMEM)
    return pl.pallas_call(
        add_kernel,
        out_shape=jax.ShapeDtypeStruct(left.shape, left.dtype),
        in_specs=[vmem, vmem] + [pl.BlockSpec(memory_space=pl.ANY)] * len(earlier),
        out_specs=vmem,
        compiler_params=pltpu.CompilerParams(vmem_limit_bytes=8 << 20),
    )(left, right, *earlier)


def add_parts_kernel(left_ref, right_ref, *out_refs):
    start = 0
    for out_ref in out_refs:
        here = slice(start, start + out_ref.shape[0])
        out_ref[...] = left_ref[here, :] + right_ref[here, :]
        start += out_ref.shape[0]


def add_parts(left, right, sizes):
    vmem = pl.BlockSpec(memory_space=pltpu.VMEM)
    return pl.pallas_call(
        add_parts_kernel,
        out_shape=tuple(jax.ShapeDtypeStruct((size, left.shape[1]), left.dtype) for size in sizes),
        in_specs=[vmem, vmem],
        out_specs=(vmem,) * len(sizes),
        compiler_params=pltpu.CompilerParams(vmem_limit_bytes=8 << 20),
    )(left, right)


def first_rows_of_next(rows):
    count = lax.axis_size("tm")
    return lax.ppermute(rows, "tm", [(i, i - 1) for i in range(1, count)])


def project_kernel(half_ref, nodes_ref, signals_ref, out_ref, onehot_ref):
    @pl.when(pl.program_id(0) == 0)
    def _():
        node = lax.broadcasted_iota(jnp.int32, onehot_ref.shape, 0).astype(jnp.float32)
        scale = 1.0 / math.sqrt(CH // NODES)
        onehot_ref[...] = jnp.where(node == nodes_ref[...], scale, 0.0).astype(jnp.bfloat16)

    out_ref[...] = lax.dot_general(
        signals_ref[...], onehot_ref[...], (((1,), (1,)), ((), ())), preferred_element_type=jnp.float32
    )


def chunk_sizes(rows):
    return [rows * quarters // sum(CHUNK_QUARTERS) for quarters in CHUNK_QUARTERS]


def project(signals, channel_nodes, half):
    rows, channels = signals.shape
    parts = [size // 2 for size in chunk_sizes(rows)]
    step = math.gcd(512, *parts)
    steps = sum(parts) // step

    def block_of(i, half):
        done, block = 0, i
        for part in parts:
            count = part // step
            block = jnp.where(i >= done, done + i + half[0] * count, block)
            done += count
        return block, 0

    grid_spec = pltpu.PrefetchScalarGridSpec(
        num_scalar_prefetch=1,
        grid=(steps,),
        in_specs=[
            pl.BlockSpec((1, channels), lambda i, half: (0, 0)),
            pl.BlockSpec((step, channels), block_of),
        ],
        out_specs=pl.BlockSpec((step, NODES), lambda i, half: (i, 0)),
        scratch_shapes=[pltpu.VMEM((NODES, channels), jnp.bfloat16)],
    )
    return pl.pallas_call(
        project_kernel,
        out_shape=jax.ShapeDtypeStruct((rows // 2, NODES), jnp.float32),
        grid_spec=grid_spec,
        compiler_params=pltpu.CompilerParams(vmem_limit_bytes=8 << 20),
    )(half, channel_nodes, signals)


def gram_kernel(stage, earlier, chan_ref, all_lags_ref, *refs):
    refs = list(refs)
    mine_ref = refs.pop(0)
    other_ref = None if stage == "own" else refs.pop(0)
    sum_in_ref, tail_ref, after_ref = (None,) * 3 if stage == "first" else [refs.pop(0) for _ in range(3)]
    del refs[:earlier]
    out_ref = refs.pop(0)
    tail_out_ref = refs.pop(0) if stage == "first" else None
    ext_ref, high_ref, low_ref, sum_ref = refs
    half = mine_ref.shape[0]
    total_lags = all_lags_ref.shape[0]
    lag_count = sum_ref.shape[1] // NODES
    lags = [all_lags_ref[lax.rem(2 * chan_ref[0] + i, total_lags)] for i in range(lag_count)]
    own_half = lax.rem(chan_ref[0], 2)
    step_rows = high_ref.shape[0]

    def rows_from(start, count):
        return pl.ds(pl.multiple_of(start, math.gcd(MAXLAG, half)), count)

    if stage == "own":
        ext_ref[rows_from((1 - own_half) * MAXLAG, half), :] = mine_ref[...]
        ext_ref[rows_from(own_half * half, MAXLAG), :] = jnp.where(own_half == 0, tail_ref[...], after_ref[...])
        begin, steps = 0, half // step_rows
    else:
        lead = 0 if stage == "first" else MAXLAG
        end = lead + 2 * half
        ext_ref[rows_from(lead + own_half * half, half), :] = mine_ref[...]
        ext_ref[rows_from(lead + (1 - own_half) * half, half), :] = other_ref[...]
        if stage == "first":
            tail_out_ref[...] = ext_ref[end - MAXLAG : end, :]
            begin, steps = 0, (end - MAXLAG) // step_rows
        else:
            ext_ref[:lead, :] = tail_ref[...]
            ext_ref[end:, :] = after_ref[...]
            begin, steps = (1 - own_half) * half, (end - half) // step_rows
    sum_ref[...] = jnp.zeros_like(sum_ref) if stage == "first" else sum_in_ref[...]
    part = 128

    def step(i, _):
        start = begin + i * step_rows
        for lag in range(lag_count):
            for row in range(0, step_rows, part):
                value = ext_ref[pl.ds(start + row + lags[lag], part), :]
                high = value.astype(jnp.bfloat16)
                high_ref[row : row + part, lag * NODES : (lag + 1) * NODES] = high
                low_ref[row : row + part, lag * NODES : (lag + 1) * NODES] = (
                    value - high.astype(jnp.float32)
                ).astype(jnp.bfloat16)

        def product(left, right):
            return lax.dot_general(left, right, CONTRACT_ROWS, preferred_element_type=jnp.float32)

        left = slice(0, 2 * NODES)
        total = product(high_ref[:, left], high_ref[...])
        total = total + product(high_ref[:, left], low_ref[...])
        total = total + product(low_ref[:, left], high_ref[...])
        sum_ref[...] += total
        sum_ref[:, left] += product(low_ref[:, left], low_ref[:, left])
        return 0

    lax.fori_loop(0, steps, step, 0)
    if stage == "rest":
        far = lag_count - 2
        for j in range(far):
            out_ref[j * NODES : (j + 1) * NODES, :] = sum_ref[:NODES, j * NODES : (j + 1) * NODES]
            place = (far + j) * NODES
            out_ref[place : place + NODES, :] = sum_ref[NODES:, (j + 1) * NODES : (j + 2) * NODES]
        which = jnp.where(4 * chan_ref[0] >= total_lags, 1, 0)
        row = pl.multiple_of(which * NODES, NODES)
        column = pl.multiple_of((far + which) * NODES, NODES)
        out_ref[2 * far * NODES :, :] = sum_ref[pl.ds(row, NODES), pl.ds(column, NODES)]
    else:
        out_ref[...] = sum_ref[...]


def gram_part(stage, chan, lags, values, carried=(), earlier=()):
    count = lags.shape[0] // 2 + 2
    half = values[0].shape[0]
    sums = jax.ShapeDtypeStruct((2 * NODES, count * NODES), jnp.float32)
    vmem = pl.BlockSpec(memory_space=pltpu.VMEM)
    smem = pl.BlockSpec(memory_space=pltpu.SMEM)
    if stage == "first":
        rows = 2 * half
        out_shape, out_specs = (sums, jax.ShapeDtypeStruct((MAXLAG, NODES), jnp.float32)), (vmem, vmem)
    elif stage == "own":
        rows = half + MAXLAG
        out_shape, out_specs = sums, vmem
    else:
        rows = 2 * half + 2 * MAXLAG
        out_shape, out_specs = jax.ShapeDtypeStruct(((2 * count - 3) * NODES, NODES), jnp.float32), vmem
    step_rows = 512
    return pl.pallas_call(
        functools.partial(gram_kernel, stage, len(earlier)),
        out_shape=out_shape,
        in_specs=[smem, smem]
        + [vmem] * (len(values) + len(carried))
        + [pl.BlockSpec(memory_space=pl.ANY)] * len(earlier),
        out_specs=out_specs,
        scratch_shapes=[
            pltpu.VMEM((rows, NODES), jnp.float32),
            pltpu.VMEM((step_rows, count * NODES), jnp.bfloat16),
            pltpu.VMEM((step_rows, count * NODES), jnp.bfloat16),
            pltpu.VMEM((2 * NODES, count * NODES), jnp.float32),
        ],
        compiler_params=pltpu.CompilerParams(vmem_limit_bytes=12 << 20),
    )(chan, lags, *values, *carried, *earlier)


def row_of(value, index):
    return jnp.broadcast_to(value[index : index + 1, :], value.shape)


def column_of(value, index):
    return jnp.broadcast_to(value[:, index : index + 1], value.shape)


def factor_block(block):
    count = len(block)
    sub = lax.broadcasted_iota(jnp.int32, (GROUP, BLOCK), 0)
    lane = lax.broadcasted_iota(jnp.int32, (GROUP, BLOCK), 1)
    state = list(block)
    result = [None] * count
    full = [None] * count
    columns = [column_of(state[0], m) for m in range(GROUP)]
    for g in range(count):
        first_lane, next_lane = GROUP * g, GROUP * (g + 1)
        here = (lane >= first_lane) & (lane < next_lane)
        span = g // SPAN
        more = g + 1 < count
        if more:
            next_columns = [column_of(state[g + 1], next_lane + m) for m in range(GROUP)]
            next_left = [column_of(state[g + 1], first_lane + m) for m in range(GROUP)]
            state[g + 1] = jnp.where(here, 0.0, state[g + 1])
        top = jnp.where(here, jnp.where(lane == sub + first_lane, 1.0, 0.0), state[g])
        diagonal = jnp.zeros_like(top)
        scale, factors, rows = [], {}, []
        pivots = [row_of(columns[m], m) for m in range(GROUP)]
        for m in range(GROUP):
            pivot = pivots[m]
            scale.append(lax.rsqrt(pivot))
            left = columns[m] * scale[m]
            for n in range(m + 1, GROUP):
                factors[m, n] = row_of(columns[m], n) * scale[m]
                pivots[n] = pivots[n] - factors[m, n] * factors[m, n]
                columns[n] = columns[n] - left * factors[m, n]
            if more:
                next_left[m] = next_left[m] * scale[m]
                for n in range(m + 1, GROUP):
                    next_left[n] = next_left[n] - next_left[m] * factors[m, n]
                for n in range(GROUP):
                    next_columns[n] = next_columns[n] - next_left[m] * row_of(next_left[m], n)
            rows.append(row_of(top, m) * scale[m])
            below = jnp.where(sub > m, left, 0.0)
            top = jnp.where(sub == m, rows[m], top - below * rows[m])
            entries = pivot * scale[m]
            for n in range(m + 1, GROUP):
                entries = jnp.where(lane == first_lane + n, factors[m, n], entries)
            diagonal = jnp.where(sub == m, entries, diagonal)
            if more:
                state[g + 1] = state[g + 1] - next_left[m] * rows[m]
        full[g] = top
        result[g] = jnp.where(lane >= next_lane, top, jnp.where(lane >= sub + first_lane, diagonal, 0.0))
        state[g] = jnp.where(lane < next_lane, top, 0.0)
        columns = next_columns
        for s in range(g + 2, min(count, (span + 2) * SPAN)):
            left = [column_of(state[s], first_lane + m) for m in range(GROUP)]
            value = jnp.where(here, 0.0, state[s])
            for m in range(GROUP):
                left[m] = left[m] * scale[m]
                for n in range(m + 1, GROUP):
                    left[n] = left[n] - left[m] * factors[m, n]
                value = value - left[m] * rows[m]
            state[s] = value
        rest = (span + 2) * SPAN
        if g % SPAN == SPAN - 1 and rest < count:
            begin = span * SPAN
            left = jnp.concatenate(full[begin : g + 1], axis=0)
            right = [
                jnp.where((lane >= GROUP * (i + 1)) & (lane < next_lane), 0.0, full[i]) for i in range(begin, g + 1)
            ]
            update = lax.dot_general(
                left[:, GROUP * rest :],
                jnp.concatenate(right, axis=0),
                CONTRACT_ROWS,
                precision=HIGHEST,
                preferred_element_type=jnp.float32,
            )
            inside = (lane >= GROUP * begin) & (lane < next_lane)
            for s in range(rest, count):
                place = GROUP * (s - rest)
                state[s] = jnp.where(inside, 0.0, state[s]) - update[place : place + GROUP]
    return result, state


def arrange(scale, layout, half_ref, mine_refs, other_refs, natural_ref, ordered_ref):
    chan_count = 4
    lag_count = 2 * chan_count
    far = lag_count // 2
    width = NODES // chan_count

    def rows_of(refs, high, start, stop):
        found, base = [], 0
        for ref, pieces in zip(refs, layout):
            for first, count, place in pieces[high]:
                low, end = max(start, base + first), min(stop, base + first + count)
                if low < end:
                    offset = place - base - first
                    found.append(ref[low + offset : end + offset, :])
            base += ref.shape[0] // 2
        return found[0] if len(found) == 1 else jnp.concatenate(found, axis=0)

    def place(refs, low):
        for high in range(2):
            chan = 2 * high + low
            pairs = [(2 * chan + i, (2 * chan + i + d) % lag_count) for i in range(2) for d in range(far)]
            odd = 2 * chan // far
            pairs.append((2 * chan + odd, (2 * chan + odd + far) % lag_count))
            for index, (left, right) in enumerate(pairs):
                block = rows_of(refs, high, index * NODES, (index + 1) * NODES)
                natural_ref[left * NODES : (left + 1) * NODES, right * NODES : (right + 1) * NODES] = block
                if left != right:
                    natural_ref[right * NODES : (right + 1) * NODES, left * NODES : (left + 1) * NODES] = block.T

    for low in range(2):

        @pl.when(half_ref[0] == low)
        def _():
            place(mine_refs, low)
            place(other_refs, 1 - low)

    lane_part = lax.broadcasted_iota(jnp.int32, (width, NODES), 1) // width

    def rows_of_lag(lag, _):
        for group in range(chan_count):
            source = pl.ds(pl.multiple_of(lag * NODES + group * width, width), width)
            target = pl.ds(pl.multiple_of(group * lag_count * width + lag * width, width), width)
            for half in range(2):
                parts = [natural_ref[source, (4 * half + i) * NODES : (4 * half + i + 1) * NODES] for i in range(4)]
                turned = []
                for shift in range(4):
                    value = parts[shift]
                    for lane in range(1, 4):
                        value = jnp.where(lane_part == lane, parts[(lane + shift) % 4], value)
                    turned.append(pltpu.roll(value, shift * width, 1) if shift else value)
                for other in range(group, chan_count):
                    block = turned[-other % 4]
                    for i in range(1, 4):
                        block = jnp.where(lane_part == i, turned[(i - other) % 4], block)
                    column = (2 * other + half) * BLOCK
                    ordered_ref[target, column : column + BLOCK] = block * scale
        return 0

    lax.fori_loop(0, lag_count, rows_of_lag, 0)


def cholesky_kernel(scale, layout, half_ref, *refs):
    parts = len(layout)
    mine_refs, other_refs = refs[:parts], refs[parts : 2 * parts]
    out_ref, natural_ref, ordered_ref, result_ref, panel_ref, inverse_ref, sent = refs[2 * parts :]
    arrange(scale, layout, half_ref, mine_refs, other_refs, natural_ref, ordered_ref)
    count = out_ref.shape[0] // BLOCK
    result_ref[...] = jnp.zeros_like(result_ref)
    panel_ref[...] = ordered_ref[:BLOCK, :]

    def send(k):
        rows = pl.ds(pl.multiple_of(k * BLOCK, BLOCK), BLOCK)
        return pltpu.make_async_copy(result_ref.at[rows, :], out_ref.at[rows, :], sent.at[k])

    def step(k, _):
        start = pl.multiple_of(k * BLOCK, BLOCK)
        block = [panel_ref[GROUP * s : GROUP * (s + 1), pl.ds(start, BLOCK)] for s in range(BLOCK // GROUP)]
        block, inverse = factor_block(block)
        for s in range(BLOCK // GROUP):
            result_ref[pl.ds(pl.multiple_of(start + GROUP * s, GROUP), GROUP), pl.ds(start, BLOCK)] = block[s]
            inverse_ref[GROUP * s : GROUP * (s + 1), :] = inverse[s]
        for kk in range(count - 1):

            @pl.when(k == kk)
            def _():
                now, later = kk * BLOCK, (kk + 1) * BLOCK
                row = jnp.dot(
                    inverse_ref[...], panel_ref[:, later:], precision=HIGHEST, preferred_element_type=jnp.float32
                )

                def product(left, right):
                    return lax.dot_general(
                        left, right, CONTRACT_ROWS, precision=HIGHEST, preferred_element_type=jnp.float32
                    )

                panel = ordered_ref[later : later + BLOCK, later:]
                if kk:
                    panel = panel - product(result_ref[:now, later : later + BLOCK], result_ref[:now, later:])
                result_ref[now:later, later:] = row
                panel_ref[:, later:] = panel - product(row[:, :BLOCK], row)

        send(k).start()
        return 0

    lax.fori_loop(0, count, step, 0)
    for k in range(count):
        send(k).wait()


def cholesky(half, mine, other, layout, size, scale):
    vmem = pl.BlockSpec(memory_space=pltpu.VMEM)
    return pl.pallas_call(
        functools.partial(cholesky_kernel, scale, layout),
        out_shape=jax.ShapeDtypeStruct((size, size), jnp.float32),
        in_specs=[pl.BlockSpec(memory_space=pltpu.SMEM)] + [vmem] * (2 * len(mine)),
        out_specs=pl.BlockSpec(memory_space=pl.ANY),
        scratch_shapes=[
            pltpu.VMEM((size, size), jnp.float32),
            pltpu.VMEM((size, size), jnp.float32),
            pltpu.VMEM((size, size), jnp.float32),
            pltpu.VMEM((BLOCK, size), jnp.float32),
            pltpu.VMEM((BLOCK, BLOCK), jnp.float32),
            pltpu.SemaphoreType.DMA((size // BLOCK,)),
        ],
        compiler_params=pltpu.CompilerParams(vmem_limit_bytes=24 << 20),
    )(half, *mine, *other)


def on_device(signals, channel_node, lag_offsets):
    chan = lax.axis_index("chan").reshape(1)
    half = chan % 2
    channel_nodes = channel_node.astype(jnp.float32).reshape(1, -1)
    send = project(signals, channel_nodes, 1 - half)
    received = swap(send, "chan", 1)
    keep = project(signals, channel_nodes, half)
    sizes = chunk_sizes(signals.shape[0])
    totals = add_parts(keep, received, [size // 2 for size in sizes])
    sent = [swap(total, "chan", 2) for total in totals]
    value = add(totals[0], sent[0])
    other = swap(value, "chan", 1)
    head = jnp.where(half[0] == 0, value[:MAXLAG], other[:MAXLAG])
    after = first_rows_of_next(head)
    sums, tail = gram_part("first", chan, lag_offsets, (value, other), earlier=(head,))
    value = add(totals[1], sent[1], tail, after)
    other = swap(value, "chan", 1)
    sums = gram_part("own", chan, lag_offsets, (value,), (sums, tail, after))
    carried = gram_part("rest", chan, lag_offsets, (value, other), (sums, tail, after))
    rows = carried.shape[0] // 2
    mine = [route.reduce(part) for route, part in zip(routes(), (carried[:rows], carried[rows:]))]
    other = [swap(value, "chan", 1) for value in mine]
    layout = [[route.pieces(rows, high) for high in range(2)] for route in routes()]
    size = lag_offsets.shape[0] * NODES
    return cholesky(half, mine, other, layout, size, 1.0 / (signals.shape[0] * lax.axis_size("tm")))


def solution(mesh):
    return jax.shard_map(
        on_device, mesh=mesh, in_specs=(P("tm", "chan"), P("chan"), P()), out_specs=P(), check_vma=False
    )
```
